128 devices in a mesh: dp: 8 (over x, y_lo), tensor: 16 (over z, y_hi, core).
Axes of the slice: x: 4, y: 4 (y_hi: 2, y_lo: 2; y = y_hi * 2 + y_lo), z: 4, core: 2. Of those that a mesh axis runs over, the one named last changes fastest.
Arguments:
- grad_parts: bfloat16 [8, 14336, 4096], P('dp', 'tensor'), may hold values from -6 to 6
- master: float32 [14336, 4096], P('tensor', 'dp'), may hold values from -0.046875 to 0.046875
- moment_one: float32 [14336, 4096], P('tensor', 'dp'), may hold values from -3 to 3
- moment_two: float32 [14336, 4096], P('tensor', 'dp'), may hold values from 0.01 to 1
- gate_act: bfloat16 [8192, 14336], P('dp', 'tensor'), may hold values from -6 to 6
- up_act: bfloat16 [8192, 14336], P('dp', 'tensor'), may hold values from -6 to 6
Outputs:
- new_master: float32 [14336, 4096], P('tensor', 'dp')
- mixed: bfloat16 [8192, 4096], P('dp')
The draws below stay inside these ranges and needn't reach their ends.
All inputs are finite; a program needn't handle non-finite values.
Results may differ from the reference program's by a relative error of at most 0.025.
Values may be sent and summed in bfloat16 or wider, within the bound.
A program may use at most 128 MiB of HBM per device.

```python
import math
import jax
import jax.numpy as jnp
from jax import lax

D = 4096
FF = 14336
TOKENS = 8192
N_DP = 8
N_TENSOR = 16


def raised(drawn, key, source, target, parts, factor):
    def block_of(axis_at):
        return (jnp.arange(drawn.shape[axis_at]) // (drawn.shape[axis_at] // parts)).reshape((-1,) + (1,) * (drawn.ndim - 1 - axis_at))

    one_side = jax.random.permutation(key, parts)[block_of(target)]
    far = (block_of(target) + parts // 2) % parts
    return jnp.where((block_of(source) == one_side) | (block_of(source) == far), factor * drawn, drawn)


def shard_levels(stream_key, dims, shards, least, largest):
    loudness = 1.0
    for axis_at, shards_of in shards:
        heights = jax.random.uniform(jax.random.fold_in(jax.random.fold_in(stream_key, 6), axis_at), (shards_of,), jnp.float32, least / len(shards), largest / len(shards))
        loudness = loudness * jnp.repeat(jnp.exp(heights), dims[axis_at] // shards_of).reshape((-1,) + (1,) * (len(dims) - 1 - axis_at))
    return loudness


def bell_draw(rng, dims, deviation, reach, pieces=(), kind=jnp.bfloat16):
    result = deviation * jax.random.normal(rng, dims, jnp.float32)
    if pieces:
        result = result * shard_levels(rng, dims, pieces, -0.22, 0.18)
    return jnp.clip(result, -reach, reach).astype(kind)


def noise_with(key, extent, width, reach, split, heavy, kind=jnp.bfloat16):
    result = width * jax.random.normal(key, extent, jnp.float32)
    if split:
        result = result * shard_levels(key, extent, split, -0.22, 0.18)
    return jnp.clip(raised(result, jax.random.fold_in(key, 3), *heavy), -reach, reach).astype(kind)


def setup_inputs(seed: int = 0) -> dict:
    streams_of = jax.random.split(jax.random.key(seed), 7)
    return {
        "grad_parts": noise_with(streams_of[0], (N_DP, FF, D), 1.0, 6.0, ((0, 8), (1, 16)), (0, 2, 8, 2.0)),
        "master": bell_draw(streams_of[1], (FF, D), FF ** -0.5, 0.046875, ((0, 16), (1, 8)), jnp.float32),
        "moment_one": bell_draw(streams_of[2], (FF, D), 0.3, 3.0, ((0, 16), (1, 8)), jnp.float32),
        "moment_two": jnp.clip(jnp.exp(math.log(1.0) - 4.6051702 * jax.random.uniform(streams_of[3], (FF, D), jnp.float32) ** shard_levels(streams_of[3], (FF, D), ((0, 16), (1, 8)), -0.2, 0.2)), 0.01, 1.0),
        "gate_act": bell_draw(streams_of[4], (TOKENS, FF), 1.0, 6.0, ((0, 8), (1, 16))),
        "up_act": bell_draw(streams_of[5], (TOKENS, FF), 1.0, 6.0, ((0, 8), (1, 16))),
    }


beta_one = 0.9
beta_two = 0.95
epsilon = 1e-08
weight_decay = 0.1
step_count = 20

def reference(grad_parts, master, moment_one, moment_two, gate_act, up_act):
    learn_rate = 0.8 / math.sqrt(FF)

    def add_part(running, partial_value):
        return (running + partial_value.astype(jnp.float32), None)
    grad_sum, _ = lax.scan(add_part, jnp.zeros(master.shape, jnp.float32), grad_parts)
    moment_new = beta_one * moment_one + (1.0 - beta_one) * grad_sum
    square_new = beta_two * moment_two + (1.0 - beta_two) * grad_sum * grad_sum
    corr_one = 1.0 - beta_one ** step_count
    corr_two = 1.0 - beta_two ** step_count
    update = moment_new / corr_one / (jnp.sqrt(square_new / corr_two) + epsilon)
    new_master = master - learn_rate * (update + weight_decay * master)
    new_weights = new_master.astype(jnp.bfloat16)
    hidden = (jax.nn.silu(gate_act.astype(jnp.float32)) * up_act.astype(jnp.float32)).astype(jnp.bfloat16)
    slab_width = FF // N_TENSOR

    def add_group(running, number):
        offset = (number * slab_width).astype(jnp.int32)
        columns = lax.dynamic_slice_in_dim(hidden, offset, slab_width, 1)
        weight_rows = lax.dynamic_slice_in_dim(new_weights, offset, slab_width, 0)
        partial_value = jnp.dot(columns, weight_rows, preferred_element_type=jnp.float32).astype(jnp.bfloat16)
        return (running + partial_value.astype(jnp.float32), None)
    total, _ = lax.scan(add_group, jnp.zeros((TOKENS, D), jnp.float32), jnp.arange(N_TENSOR, dtype=jnp.int32))
    return (new_master, total.astype(jnp.bfloat16))
```

```python
import functools
import math

import jax
import jax.numpy as jnp
from jax import lax
from jax.experimental import pallas as pl
from jax.experimental.pallas import tpu as pltpu
from jax.sharding import PartitionSpec as P

FF = 14336

beta_one = 0.9
beta_two = 0.95
epsilon = 1e-08
weight_decay = 0.1
step_count = 20

MESH = pl.DeviceIdType.MESH
F32 = jnp.float32
BF16 = jnp.bfloat16

K = 4
LANES = 128
HP = 8


def sweep(rows, tile, body):
    if rows == tile:
        body(0)
        return

    @pl.loop(0, rows // tile)
    def _(i):
        body(pl.multiple_of(i * tile, tile))


def kernel(
    g, mst, mom, sqr, gate, up,
    nm_out, mix_out,
    gown, gfw, r1, r2, sy, ry, mst_v, mom_v, sqr_v, w, gate_v, up_v, hid,
    p, rc, zr1, zr2, yb, yr, out,
    ld, nms, outs_sem,
    x1s, x1r, rws, rwr, x2s, x2r, ys, yrs, a1s, a1r, a2s, a2r, hs, hr,
    cs, cr, z1s, z1r, zws, zwr, z2s, z2r, y3s, y3r, o1s, o1r, o2s, o2r, ocs, ocr,
):
    dp, t = lax.axis_index("dp"), lax.axis_index("tensor")
    x, yl = lax.div(dp, 2), lax.rem(dp, 2)
    z, yh, c = lax.div(t, 4), lax.rem(lax.div(t, 2), 2), lax.rem(t, 2)
    xn, xp = lax.rem(x + 1, 4), lax.rem(x + 3, 4)
    xo = lax.rem(x + 2, 4)
    zn, zp = lax.rem(z + 1, 4), lax.rem(z + 3, 4)
    zo = lax.rem(z + 2, 4)

    def dev(x=x, yl=yl, z=z, yh=yh, c=c):
        return (x * 2 + yl, z * 4 + yh * 2 + c)

    X = (dev(x=xn), dev(x=xp))
    Z = (dev(z=zn), dev(z=zp))
    YL = dev(yl=1 - yl)
    YH = dev(yh=1 - yh)
    YD = dev(yl=1 - yl, yh=1 - yh)
    C = dev(c=1 - c)

    rows = gown.shape[1]
    half = rows // 2
    tokens = hid.shape[1]
    wide = p.shape[3]
    core_rows = tokens // 2
    zrows = core_rows // 4
    zh = zrows // 2

    sends = []
    done = {}

    def remote(src, dst, s, r, to):
        cp = pltpu.make_async_remote_copy(
            src_ref=src, dst_ref=dst, send_sem=s, recv_sem=r, device_id=to, device_id_type=MESH
        )
        cp.start()
        sends.append(cp)
        return cp

    def columns(owner, strip, k, width=LANES):
        return pl.ds(pl.multiple_of(owner * (2 * K * LANES) + strip * (K * LANES) + k * LANES, LANES), width)

    loads = {}

    def load(name, i, src, dst):
        cp = pltpu.make_async_copy(src, dst, ld.at[i])
        cp.start()
        loads[name] = cp

    block = K * LANES
    load("f0", 0, g.at[0, :, columns(xn, 0, 0, block)], gfw.at[0])
    load("f1", 1, g.at[0, :, columns(xp, 1, 0, block)], gfw.at[1])
    load("gate", 2, gate, gate_v)
    load("up", 3, up, up_v)
    load("own0", 4, g.at[0, :, columns(x, 0, 0, block)], gown.at[0])
    load("own1", 5, g.at[0, :, columns(x, 1, 0, block)], gown.at[1])
    load("mst", 6, mst, mst_v)
    load("mom", 7, mom, mom_v)
    load("sqr", 8, sqr, sqr_v)

    def loaded(*names):
        for n in names:
            if n in loads:
                loads.pop(n).wait()

    barrier = pltpu.get_barrier_semaphore()
    friends = (*X, *Z, YL, YH, YD, C)
    for d in friends:
        pl.semaphore_signal(barrier, inc=1, device_id=d, device_id_type=MESH)
    pl.semaphore_wait(barrier, len(friends))

    def X1(k):
        done["x1", 0, k] = remote(
            g.at[0, :, columns(xo, 0, k)], r1.at[0, k], x1s.at[0, k], x1r.at[0, k], X[0])
        done["x1", 1, k] = remote(
            g.at[0, :, columns(xo, 1, k)], r1.at[1, k], x1s.at[1, k], x1r.at[1, k], X[1])

    def R(k):
        done["rw", 0, k] = remote(
            g.at[0, :, columns(xn, 1, k)], r2.at[0, k, 1], rws.at[0, k], rwr.at[0, k], X[0])
        done["rw", 1, k] = remote(
            g.at[0, :, columns(xp, 0, k)], r2.at[1, k, 0], rws.at[1, k], rwr.at[1, k], X[1])

    def X2(k):
        loaded("f0", "f1")
        cols = pl.ds(k * LANES, LANES)
        for d in (0, 1):
            done["x1", d, k].wait_recv()

            def body(r):
                at = pl.ds(r, 128)
                gfw[d, at, cols] = (gfw[d, at, cols].astype(F32) + r1[d, k, at, :].astype(F32)).astype(BF16)

            sweep(rows, 128, body)
            done["x2", d, k] = remote(
                gfw.at[d, :, cols], r2.at[d, k, d], x2s.at[d, k], x2r.at[d, k], X[d])

    def X3(k):
        loaded("own0", "own1")
        for d in (0, 1):
            done["rw", d, k].wait_recv()
            done["x2", d, k].wait_recv()
        cols = pl.ds(k * LANES, LANES)
        other = 1 - yl

        def body(r):
            at = pl.ds(r, 128)
            sy[k, at, :] = (
                gown[other, at, cols].astype(F32)
                + r2[0, k, other, at, :].astype(F32)
                + r2[1, k, other, at, :].astype(F32)
            ).astype(BF16)

        sweep(rows, 128, body)
        done["y", k] = remote(sy.at[k], ry.at[k], ys.at[k], yrs.at[k], YL)

    learn_rate = 0.8 / math.sqrt(FF)
    corr_one = 1.0 - beta_one**step_count
    corr_two = 1.0 - beta_two**step_count

    def Y1(k):
        loaded("mst", "mom", "sqr")
        done["y", k].wait_recv()
        cols = pl.ds(k * LANES, LANES)

        def body(r):
            at = pl.ds(r, 64)
            grad = (
                gown[yl, at, cols].astype(F32)
                + r2[0, k, yl, at, :].astype(F32)
                + r2[1, k, yl, at, :].astype(F32)
                + ry[k, at, :].astype(F32)
            )
            moment_new = beta_one * mom_v[at, cols] + (1.0 - beta_one) * grad
            square_new = beta_two * sqr_v[at, cols] + (1.0 - beta_two) * grad * grad
            update = moment_new / corr_one / (jnp.sqrt(square_new / corr_two) + epsilon)
            old = mst_v[at, cols]
            new = old - learn_rate * (update + weight_decay * old)
            mst_v[at, cols] = new
            w[k, x, at, :] = new.astype(BF16)

        sweep(rows, 64, body)
        for d in (0, 1):
            done["a1", d, k] = remote(
                w.at[k, x], w.at[k, x], a1s.at[d, k], a1r.at[d, k], X[d])
        cp = pltpu.make_async_copy(mst_v.at[:, cols], nm_out.at[:, cols], nms.at[k])
        cp.start()
        done["nm", k] = cp

    def A2(k):
        for d, origin in ((0, xp), (1, xn)):
            done["a1", d, k].wait_recv()
            at = pl.ds(d * half, half)
            done["a2", d, k] = remote(
                w.at[k, origin, at], w.at[k, origin, at], a2s.at[d, k], a2r.at[d, k], X[d])

    piece = tokens // HP

    def HID():
        loaded("gate", "up")

        def body(r):
            at = pl.ds(r, 32)
            v = gate_v[at, :].astype(F32)
            hid[0, at, :] = (v / (1.0 + jnp.exp(-v)) * up_v[at, :].astype(F32)).astype(BF16)

        sweep(tokens, 32, body)

    def H(i):
        at = pl.ds(i * piece, piece)
        done["h", i] = remote(hid.at[0, at], hid.at[1, at], hs.at[i], hr.at[i], YL)

    def M(k, h):
        if h == 0:
            for d in (0, 1):
                done["a2", d, k].wait_recv()
        elif k == 0:
            for i in range(HP):
                done["h", i].wait_recv()
        for part in (1 - c, c):
            def body(r):
                at = pl.ds(pl.multiple_of(part * core_rows + r, 256), 256)
                weights = jnp.concatenate([w[k, j] for j in range(4)], axis=1)
                p[k, h, at, :] = jnp.dot(
                    hid[h, at, :], weights, preferred_element_type=F32).astype(BF16)

            sweep(core_rows, 256, body)
            if part is not c:
                at = pl.ds(pl.multiple_of((1 - c) * core_rows, core_rows), core_rows)
                done["c", k, h] = remote(p.at[k, h, at], rc.at[k, h], cs.at[k, h], cr.at[k, h], C)

    base = c * core_rows

    def zat(owner, part, count):
        return pl.ds(pl.multiple_of(base + owner * zrows + part * zh, zh), count)

    def Z0(k, h):
        done["c", k, h].wait_recv()

        def body(r):
            at = pl.ds(pl.multiple_of(base + r, 64), 64)
            p[k, h, at, :] = (p[k, h, at, :].astype(F32) + rc[k, h, pl.ds(r, 64), :].astype(F32)).astype(BF16)

        sweep(core_rows, 64, body)
        for d in (0, 1):
            done["z1", d, k, h] = remote(
                p.at[k, h, zat(zo, d, zh)], zr1.at[d, k, h], z1s.at[d, k, h], z1r.at[d, k, h], Z[d])
        for d, owner in ((0, zn), (1, zp)):
            done["zw", d, k, h] = remote(
                p.at[k, h, zat(owner, 1 - d, zh)], zr2.at[d, k, h, pl.ds((1 - d) * zh, zh)],
                zws.at[d, k, h], zwr.at[d, k, h], Z[d])

    def Z2(k, h):
        for d, owner in ((0, zn), (1, zp)):
            done["z1", d, k, h].wait_recv()
            at = zat(owner, d, zh)
            p[k, h, at, :] = (p[k, h, at, :].astype(F32) + zr1[d, k, h].astype(F32)).astype(BF16)
            done["z2", d, k, h] = remote(
                p.at[k, h, at], zr2.at[d, k, h, pl.ds(d * zh, zh)], z2s.at[d, k, h], z2r.at[d, k, h], Z[d])

    def Z3(k, h):
        for d in (0, 1):
            done["zw", d, k, h].wait_recv()
            done["z2", d, k, h].wait_recv()
        for part in (0, 1):
            at = pl.ds(part * zh, zh)
            yb[k, h, at, :] = (
                p[k, h, zat(z, part, zh), :].astype(F32)
                + zr2[0, k, h, at, :].astype(F32)
                + zr2[1, k, h, at, :].astype(F32)
            ).astype(BF16)
        for i, to in ((0, YH),) if h == 0 else ((1, YL), (2, YD)):
            done["y3", k, i] = remote(yb.at[k, h], yr.at[k, i], y3s.at[k, i], y3r.at[k, i], to)

    def oat(owner, part, count):
        return pl.ds(pl.multiple_of(base + owner * zrows + part * zh, zh), count)

    def Y2(k, h):
        group = yl if h == 0 else 1 - yl
        for i in (0,) if h == 0 else (1, 2):
            done["y3", k, i].wait_recv()
        for part in (0, 1):
            at = pl.ds(part * zh, zh)
            if h == 0:
                total = yb[k, 0, at, :].astype(F32) + yr[k, 0, at, :].astype(F32)
            else:
                total = yr[k, 1, at, :].astype(F32) + yr[k, 2, at, :].astype(F32)
            out[k, group, oat(z, part, zh), :] = total.astype(BF16)
        mine = out.at[k, group, oat(z, 0, zrows)]
        for d in (0, 1):
            done["o1", d, k, h] = remote(mine, mine, o1s.at[d, k, h], o1r.at[d, k, h], Z[d])

    def O2(k, h):
        group = yl if h == 0 else 1 - yl
        for d, origin in ((0, zp), (1, zn)):
            done["o1", d, k, h].wait_recv()
            part = out.at[k, group, oat(origin, d, zh)]
            done["o2", d, k, h] = remote(part, part, o2s.at[d, k, h], o2r.at[d, k, h], Z[d])

    def O3(k, h):
        group = yl if h == 0 else 1 - yl
        for d in (0, 1):
            done["o2", d, k, h].wait_recv()
        part = out.at[k, group, pl.ds(pl.multiple_of(base, core_rows), core_rows)]
        done["oc", k, h] = remote(part, part, ocs.at[k, h], ocr.at[k, h], C)

    def E(k, h):
        group = yl if h == 0 else 1 - yl
        done["oc", k, h].wait_recv()
        for j in range(4):
            cp = pltpu.make_async_copy(
                out.at[k, group, :, pl.ds(j * LANES, LANES)],
                mix_out.at[:, columns(j, group, k)], outs_sem.at[k, h, j])
            cp.start()
            done["e", k, h, j] = cp

    X1(0), R(0)
    HID()
    H(0), H(1), H(2)
    X2(0), X1(1), R(1)
    X3(0), H(3), H(4)
    X2(1), X1(2)
    Y1(0)
    R(2), H(5)
    X3(1)
    A2(0)
    H(6), H(7)
    X2(2), X1(3)
    M(0, 0)
    Y1(1)
    R(3)
    Z0(0, 0)
    A2(1)
    Z2(0, 0)
    X3(2)
    M(0, 1)
    Z3(0, 0)
    Z0(0, 1)
    X2(3)
    Y2(0, 0)
    M(1, 0)
    Z2(0, 1)
    Z0(1, 0)
    Y1(2)
    O2(0, 0)
    Z3(0, 1)
    M(1, 1)
    Z2(1, 0)
    Z0(1, 1)
    Y2(0, 1)
    O3(0, 0)
    X3(3)
    A2(2)
    Z3(1, 0)
    Z2(1, 1)
    O2(0, 1)
    E(0, 0)
    Y2(1, 0)
    Z3(1, 1)
    O3(0, 1)
    Y1(3)
    M(2, 0)
    Z0(2, 0)
    O2(1, 0)
    Y2(1, 1)
    M(2, 1)
    Z0(2, 1)
    A2(3)
    E(0, 1)
    Z2(2, 0)
    O3(1, 0)
    O2(1, 1)
    Z2(2, 1)
    Z3(2, 0)
    M(3, 0)
    Z0(3, 0)
    Z3(2, 1)
    M(3, 1)
    Z0(3, 1)
    Y2(2, 0)
    E(1, 0)
    O3(1, 1)
    Z2(3, 0)
    Y2(2, 1)
    O2(2, 0)
    Z2(3, 1)
    Z3(3, 0)
    E(1, 1)
    O2(2, 1)
    O3(2, 0)
    Z3(3, 1)
    Y2(3, 0)
    O3(2, 1)
    E(2, 0)
    Y2(3, 1)
    O2(3, 0)
    E(2, 1)
    O2(3, 1)
    O3(3, 0)
    O3(3, 1)
    E(3, 0)
    E(3, 1)

    for cp in sends:
        cp.wait_send()
    for key, cp in done.items():
        if key[0] in ("nm", "e"):
            cp.wait()


def per_device(grad_parts, master, moment_one, moment_two, gate_act, up_act):
    _, rows, width = grad_parts.shape
    tokens = gate_act.shape[0]
    hbm = pl.BlockSpec(memory_space=pl.ANY)
    block = K * LANES
    vm = pltpu.VMEM
    dma = pltpu.SemaphoreType.DMA

    def pair(shape):
        return [dma(shape), dma(shape)]

    return pl.pallas_call(
        kernel,
        out_shape=(
            jax.ShapeDtypeStruct(master.shape, F32),
            jax.ShapeDtypeStruct((tokens, width), BF16),
        ),
        in_specs=[hbm] * 6,
        out_specs=(hbm, hbm),
        scratch_shapes=[
            vm((2, rows, block), BF16),
            vm((2, rows, block), BF16),
            vm((2, K, rows, LANES), BF16),
            vm((2, K, 2, rows, LANES), BF16),
            vm((K, rows, LANES), BF16),
            vm((K, rows, LANES), BF16),
            vm((rows, block), F32),
            vm((rows, block), F32),
            vm((rows, block), F32),
            vm((K, 4, rows, LANES), BF16),
            vm((tokens, rows), BF16),
            vm((tokens, rows), BF16),
            vm((2, tokens, rows), BF16),
            vm((K, 2, tokens, block), BF16),
            vm((K, 2, tokens // 2, block), BF16),
            vm((2, K, 2, tokens // 16, block), BF16),
            vm((2, K, 2, tokens // 8, block), BF16),
            vm((K, 2, tokens // 8, block), BF16),
            vm((K, 3, tokens // 8, block), BF16),
            vm((K, 2, tokens, block), BF16),
            dma((9,)), dma((K,)), dma((K, 2, 4)),
            *pair((2, K)), *pair((2, K)), *pair((2, K)), *pair((K,)),
            *pair((2, K)), *pair((2, K)), *pair((HP,)),
            *pair((K, 2)), *pair((2, K, 2)), *pair((2, K, 2)), *pair((2, K, 2)),
            *pair((K, 3)), *pair((2, K, 2)), *pair((2, K, 2)), *pair((K, 2)),
        ],
        compiler_params=pltpu.CompilerParams(
            collective_id=0, has_side_effects=True, vmem_limit_bytes=62 * 2**20
        ),
        name="handover",
    )(grad_parts, master, moment_one, moment_two, gate_act, up_act)


def solution(mesh):
    in_specs = (
        P("dp", "tensor", None),
        P("tensor", "dp"),
        P("tensor", "dp"),
        P("tensor", "dp"),
        P("dp", "tensor"),
        P("dp", "tensor"),
    )
    out_specs = (P("tensor", "dp"), P("dp", None))
    return jax.shard_map(
        per_device, mesh=mesh, in_specs=in_specs, out_specs=out_specs, check_vma=False
    )
```

```python
import functools
import math

import jax
import jax.numpy as jnp
from jax import lax
from jax.experimental import pallas as pl
from jax.experimental.pallas import tpu as pltpu
from jax.sharding import PartitionSpec as P

FF = 14336

beta_one = 0.9
beta_two = 0.95
epsilon = 1e-08
weight_decay = 0.1
step_count = 20

MESH = pl.DeviceIdType.MESH
F32 = jnp.float32
BF16 = jnp.bfloat16

K = 4
LANES = 128
HP = 8


def sweep(rows, tile, body):
    if rows == tile:
        body(0)
        return

    @pl.loop(0, rows // tile)
    def _(i):
        body(pl.multiple_of(i * tile, tile))


def plan():
    return [
        ("X1", 2), ("R", 3), ("HID",), ("X1", 3), ("H", 0), ("H", 4), ("H", 2), ("R", 2), ("X2", 2), ("X2", 3),
        ("H", 6), ("X1", 1), ("X3", 2), ("X3", 3), ("H", 1), ("H", 3), ("H", 5), ("Y1", 2), ("Y1", 3),
        ("A2", 2), ("A2", 3), ("R", 1), ("X2", 1), ("X1", 0), ("H", 7), ("M", 2, 0), ("M", 3, 0), ("Z0", 2, 0),
        ("Z0", 3, 0), ("M", 2, 1), ("R", 0), ("Z2", 2, 0), ("X3", 1), ("Z2", 3, 0), ("Z0", 2, 1), ("M", 3, 1),
        ("Z3", 2, 0), ("Z2", 2, 1), ("Z3", 3, 0), ("X2", 0), ("Z0", 3, 1), ("Z3", 2, 1), ("Y2", 2, 0),
        ("Y1", 1), ("Y2", 3, 0), ("X3", 0), ("Z2", 3, 1), ("Y2", 2, 1), ("O2", 2, 0), ("O2", 3, 0), ("A2", 1),
        ("Z3", 3, 1), ("Y1", 0), ("O2", 2, 1), ("M", 1, 0), ("Y2", 3, 1), ("M", 1, 1), ("Z0", 1, 0), ("A2", 0),
        ("Z0", 1, 1), ("O2", 3, 1), ("M", 0, 0), ("Z2", 1, 0), ("Z2", 1, 1), ("M", 0, 1), ("Z0", 0, 0),
        ("Z3", 1, 0), ("O3", 3, 1), ("Z0", 0, 1), ("Z3", 1, 1), ("E", 3, 1), ("Z2", 0, 0), ("Z2", 0, 1),
        ("O3", 2, 0), ("O3", 2, 1), ("Y2", 1, 0), ("Z3", 0, 0), ("Y2", 1, 1), ("Z3", 0, 1), ("O2", 1, 0),
        ("Y2", 0, 0), ("O3", 3, 0), ("E", 2, 0), ("Y2", 0, 1), ("O2", 1, 1), ("O3", 1, 0), ("E", 2, 1),
        ("O2", 0, 0), ("E", 3, 0), ("O2", 0, 1), ("O3", 1, 1), ("O3", 0, 0), ("O3", 0, 1), ("E", 0, 0),
        ("E", 1, 0), ("E", 1, 1), ("E", 0, 1),
    ]


def kernel(
    g, mst, mom, sqr, gate, up,
    mst_v, out,
    gown, gfw, r1, r2, sy, ry, mom_v, sqr_v, w, gate_v, up_v, hid,
    p, rc, zr1, zr2, yb, yr,
    ld,
    x1s, x1r, rws, rwr, x2s, x2r, ys, yrs, a1s, a1r, a2s, a2r, hs, hr,
    cs, cr, z1s, z1r, zws, zwr, z2s, z2r, y3s, y3r, o1s, o1r, o2s, o2r, ocs, ocr,
):
    dp, t = lax.axis_index("dp"), lax.axis_index("tensor")
    x, yl = lax.div(dp, 2), lax.rem(dp, 2)
    z, yh, c = lax.div(t, 4), lax.rem(lax.div(t, 2), 2), lax.rem(t, 2)
    xn, xp = lax.rem(x + 1, 4), lax.rem(x + 3, 4)
    xo = lax.rem(x + 2, 4)
    zn, zp = lax.rem(z + 1, 4), lax.rem(z + 3, 4)
    zo = lax.rem(z + 2, 4)

    def dev(x=x, yl=yl, z=z, yh=yh, c=c):
        return (x * 2 + yl, z * 4 + yh * 2 + c)

    X = (dev(x=xn), dev(x=xp))
    Z = (dev(z=zn), dev(z=zp))
    YL = dev(yl=1 - yl)
    YH = dev(yh=1 - yh)
    YD = dev(yl=1 - yl, yh=1 - yh)
    C = dev(c=1 - c)

    rows = gown.shape[1]
    half = rows // 2
    tokens = hid.shape[1]
    wide = p.shape[3]
    core_rows = tokens // 2
    zrows = core_rows // 4
    zh = zrows // 2

    sends = []
    done = {}

    def remote(src, dst, s, r, to):
        cp = pltpu.make_async_remote_copy(
            src_ref=src, dst_ref=dst, send_sem=s, recv_sem=r, device_id=to, device_id_type=MESH
        )
        cp.start()
        sends.append(cp)
        return cp

    def columns(owner, strip, k, width=LANES):
        return pl.ds(pl.multiple_of(owner * (2 * K * LANES) + strip * (K * LANES) + k * LANES, LANES), width)

    loads = {}

    def load(name, i, src, dst):
        cp = pltpu.make_async_copy(src, dst, ld.at[i])
        cp.start()
        loads[name] = cp

    block = K * LANES
    load("f0", 0, g.at[0, :, columns(xn, 0, 0, block)], gfw.at[0])
    load("f1", 1, g.at[0, :, columns(xp, 1, 0, block)], gfw.at[1])
    load("gate", 2, gate, gate_v)
    load("up", 3, up, up_v)
    load("own0", 4, g.at[0, :, columns(x, 0, 0, block)], gown.at[0])
    load("own1", 5, g.at[0, :, columns(x, 1, 0, block)], gown.at[1])
    load("mst", 6, mst, mst_v)
    load("mom", 7, mom, mom_v)
    load("sqr", 8, sqr, sqr_v)

    def loaded(*names):
        for n in names:
            if n in loads:
                loads.pop(n).wait()

    barrier = pltpu.get_barrier_semaphore()
    friends = (*X, *Z, YL, YH, YD, C)
    for d in friends:
        pl.semaphore_signal(barrier, inc=1, device_id=d, device_id_type=MESH)
    pl.semaphore_wait(barrier, len(friends))

    def X1(k):
        done["x1", 0, k] = remote(
            g.at[0, :, columns(xo, 0, k)], r1.at[0, k], x1s.at[0, k], x1r.at[0, k], X[0])
        done["x1", 1, k] = remote(
            g.at[0, :, columns(xo, 1, k)], r1.at[1, k], x1s.at[1, k], x1r.at[1, k], X[1])

    def R(k):
        done["rw", 0, k] = remote(
            g.at[0, :, columns(xn, 1, k)], r2.at[0, k, 1], rws.at[0, k], rwr.at[0, k], X[0])
        done["rw", 1, k] = remote(
            g.at[0, :, columns(xp, 0, k)], r2.at[1, k, 0], rws.at[1, k], rwr.at[1, k], X[1])

    def X2(k):
        loaded("f0", "f1")
        cols = pl.ds(k * LANES, LANES)
        for d in (0, 1):
            done["x1", d, k].wait_recv()

            def body(r):
                at = pl.ds(r, 128)
                gfw[d, at, cols] = (gfw[d, at, cols].astype(F32) + r1[d, k, at, :].astype(F32)).astype(BF16)

            sweep(rows, 128, body)
            done["x2", d, k] = remote(
                gfw.at[d, :, cols], r2.at[d, k, d], x2s.at[d, k], x2r.at[d, k], X[d])

    def X3(k):
        loaded("own0", "own1")
        for d in (0, 1):
            done["rw", d, k].wait_recv()
            done["x2", d, k].wait_recv()
        cols = pl.ds(k * LANES, LANES)
        other = 1 - yl

        def body(r):
            at = pl.ds(r, 128)
            sy[k, at, :] = (
                gown[other, at, cols].astype(F32)
                + r2[0, k, other, at, :].astype(F32)
                + r2[1, k, other, at, :].astype(F32)
            ).astype(BF16)

        sweep(rows, 128, body)
        done["y", k] = remote(sy.at[k], ry.at[k], ys.at[k], yrs.at[k], YL)

    learn_rate = 0.8 / math.sqrt(FF)
    corr_one = 1.0 - beta_one**step_count
    corr_two = 1.0 - beta_two**step_count

    def Y1(k):
        loaded("mst", "mom", "sqr")
        done["y", k].wait_recv()
        cols = pl.ds(k * LANES, LANES)

        def body(r):
            at = pl.ds(r, 64)
            grad = (
                gown[yl, at, cols].astype(F32)
                + r2[0, k, yl, at, :].astype(F32)
                + r2[1, k, yl, at, :].astype(F32)
                + ry[k, at, :].astype(F32)
            )
            moment_new = beta_one * mom_v[at, cols] + (1.0 - beta_one) * grad
            square_new = beta_two * sqr_v[at, cols] + (1.0 - beta_two) * grad * grad
            update = moment_new / corr_one / (jnp.sqrt(square_new / corr_two) + epsilon)
            old = mst_v[at, cols]
            new = old - learn_rate * (update + weight_decay * old)
            mst_v[at, cols] = new
            w[k, x, at, :] = new.astype(BF16)

        sweep(rows, 64, body)
        for d in (0, 1):
            done["a1", d, k] = remote(
                w.at[k, x], w.at[k, x], a1s.at[d, k], a1r.at[d, k], X[d])

    def A2(k):
        for d, origin in ((0, xp), (1, xn)):
            done["a1", d, k].wait_recv()
            at = pl.ds(d * half, half)
            done["a2", d, k] = remote(
                w.at[k, origin, at], w.at[k, origin, at], a2s.at[d, k], a2r.at[d, k], X[d])

    piece = tokens // HP

    def HID():
        loaded("gate", "up")

        def body(r):
            at = pl.ds(r, 32)
            v = gate_v[at, :].astype(F32)
            hid[0, at, :] = (v / (1.0 + jnp.exp(-v)) * up_v[at, :].astype(F32)).astype(BF16)

        sweep(tokens, 32, body)

    def H(i):
        at = pl.ds(i * piece, piece)
        done["h", i] = remote(hid.at[0, at], hid.at[1, at], hs.at[i], hr.at[i], YL)

    def M(k, h):
        if h == 0:
            for d in (0, 1):
                done["a2", d, k].wait_recv()
        elif ("h", 0) in done:
            for i in range(HP):
                done.pop(("h", i)).wait_recv()
        for part in (1 - c, c):
            def body(r):
                at = pl.ds(pl.multiple_of(part * core_rows + r, 256), 256)
                weights = jnp.concatenate([w[k, j] for j in range(4)], axis=1)
                p[k, h, at, :] = jnp.dot(
                    hid[h, at, :], weights, preferred_element_type=F32).astype(BF16)

            sweep(core_rows, 256, body)
            if part is not c:
                at = pl.ds(pl.multiple_of((1 - c) * core_rows, core_rows), core_rows)
                done["c", k, h] = remote(p.at[k, h, at], rc.at[k, h], cs.at[k, h], cr.at[k, h], C)

    base = c * core_rows

    def zat(owner, part, count):
        return pl.ds(pl.multiple_of(base + owner * zrows + part * zh, zh), count)

    def Z0(k, h):
        done["c", k, h].wait_recv()

        def body(r):
            at = pl.ds(pl.multiple_of(base + r, 64), 64)
            p[k, h, at, :] = (p[k, h, at, :].astype(F32) + rc[k, h, pl.ds(r, 64), :].astype(F32)).astype(BF16)

        sweep(core_rows, 64, body)
        for d in (0, 1):
            done["z1", d, k, h] = remote(
                p.at[k, h, zat(zo, d, zh)], zr1.at[d, k, h], z1s.at[d, k, h], z1r.at[d, k, h], Z[d])
        for d, owner in ((0, zn), (1, zp)):
            done["zw", d, k, h] = remote(
                p.at[k, h, zat(owner, 1 - d, zh)], zr2.at[d, k, h, pl.ds((1 - d) * zh, zh)],
                zws.at[d, k, h], zwr.at[d, k, h], Z[d])

    def Z2(k, h):
        for d, owner in ((0, zn), (1, zp)):
            done["z1", d, k, h].wait_recv()
            at = zat(owner, d, zh)
            p[k, h, at, :] = (p[k, h, at, :].astype(F32) + zr1[d, k, h].astype(F32)).astype(BF16)
            done["z2", d, k, h] = remote(
                p.at[k, h, at], zr2.at[d, k, h, pl.ds(d * zh, zh)], z2s.at[d, k, h], z2r.at[d, k, h], Z[d])

    def Z3(k, h):
        for d in (0, 1):
            done["zw", d, k, h].wait_recv()
            done["z2", d, k, h].wait_recv()
        for part in (0, 1):
            at = pl.ds(part * zh, zh)
            yb[k, h, at, :] = (
                p[k, h, zat(z, part, zh), :].astype(F32)
                + zr2[0, k, h, at, :].astype(F32)
                + zr2[1, k, h, at, :].astype(F32)
            ).astype(BF16)
        for i, to in ((0, YH),) if h == 0 else ((1, YL), (2, YD)):
            done["y3", k, i] = remote(yb.at[k, h], yr.at[k, i], y3s.at[k, i], y3r.at[k, i], to)

    def oat(owner, part, count):
        return pl.ds(pl.multiple_of(base + owner * zrows + part * zh, zh), count)

    def Y2(k, h):
        group = yl if h == 0 else 1 - yl
        for i in (0,) if h == 0 else (1, 2):
            done["y3", k, i].wait_recv()
        for part in (0, 1):
            at = pl.ds(part * zh, zh)
            if h == 0:
                total = yb[k, 0, at, :].astype(F32) + yr[k, 0, at, :].astype(F32)
            else:
                total = yr[k, 1, at, :].astype(F32) + yr[k, 2, at, :].astype(F32)
            out[k, group, oat(z, part, zh), :] = total.astype(BF16)
        mine = out.at[k, group, oat(z, 0, zrows)]
        for d in (0, 1):
            done["o1", d, k, h] = remote(mine, mine, o1s.at[d, k, h], o1r.at[d, k, h], Z[d])

    def O2(k, h):
        group = yl if h == 0 else 1 - yl
        for d, origin in ((0, zp), (1, zn)):
            done["o1", d, k, h].wait_recv()
            part = out.at[k, group, oat(origin, d, zh)]
            done["o2", d, k, h] = remote(part, part, o2s.at[d, k, h], o2r.at[d, k, h], Z[d])

    def O3(k, h):
        group = yl if h == 0 else 1 - yl
        for d in (0, 1):
            done["o2", d, k, h].wait_recv()
        part = out.at[k, group, pl.ds(pl.multiple_of(base, core_rows), core_rows)]
        done["oc", k, h] = remote(part, part, ocs.at[k, h], ocr.at[k, h], C)

    def E(k, h):
        done["oc", k, h].wait_recv()

    steps = dict(X1=X1, R=R, X2=X2, X3=X3, Y1=Y1, A2=A2, HID=HID, H=H, M=M, Z0=Z0, Z2=Z2, Z3=Z3, Y2=Y2, O2=O2, O3=O3, E=E)
    for name, *at in plan():
        steps[name](*at)

    for cp in sends:
        cp.wait_send()


def place(nm, out, nm_out, mix_out, sems):
    copies = [pltpu.make_async_copy(nm, nm_out, sems.at[0])]
    for k in range(K):
        for group in (0, 1):
            for j in range(4):
                at = pl.ds((j * 2 * K + group * K + k) * LANES, LANES)
                copies.append(pltpu.make_async_copy(
                    out.at[k, group, :, pl.ds(j * LANES, LANES)], mix_out.at[:, at], sems.at[len(copies)]))
    for cp in copies:
        cp.start()
    for cp in copies:
        cp.wait()


def per_device(grad_parts, master, moment_one, moment_two, gate_act, up_act):
    _, rows, width = grad_parts.shape
    tokens = gate_act.shape[0]
    hbm = pl.BlockSpec(memory_space=pl.ANY)
    block = K * LANES
    vm = pltpu.VMEM
    dma = pltpu.SemaphoreType.DMA

    def pair(shape):
        return [dma(shape), dma(shape)]

    new_master, mixed = pl.pallas_call(
        kernel,
        out_shape=(
            vm(master.shape, F32),
            vm((K, 2, tokens, block), BF16),
        ),
        in_specs=[hbm] * 6,
        scratch_shapes=[
            vm((2, rows, block), BF16),
            vm((2, rows, block), BF16),
            vm((2, K, rows, LANES), BF16),
            vm((2, K, 2, rows, LANES), BF16),
            vm((K, rows, LANES), BF16),
            vm((K, rows, LANES), BF16),
            vm((rows, block), F32),
            vm((rows, block), F32),
            vm((K, 4, rows, LANES), BF16),
            vm((tokens, rows), BF16),
            vm((tokens, rows), BF16),
            vm((2, tokens, rows), BF16),
            vm((K, 2, tokens, block), BF16),
            vm((K, 2, tokens // 2, block), BF16),
            vm((2, K, 2, tokens // 16, block), BF16),
            vm((2, K, 2, tokens // 8, block), BF16),
            vm((K, 2, tokens // 8, block), BF16),
            vm((K, 3, tokens // 8, block), BF16),
            dma((9,)),
            *pair((2, K)), *pair((2, K)), *pair((2, K)), *pair((K,)),
            *pair((2, K)), *pair((2, K)), *pair((HP,)),
            *pair((K, 2)), *pair((2, K, 2)), *pair((2, K, 2)), *pair((2, K, 2)),
            *pair((K, 3)), *pair((2, K, 2)), *pair((2, K, 2)), *pair((K, 2)),
        ],
        compiler_params=pltpu.CompilerParams(
            collective_id=0, has_side_effects=True, vmem_limit_bytes=50 * 2**20
        ),
        name="handover",
    )(grad_parts, master, moment_one, moment_two, gate_act, up_act)
    return pl.pallas_call(
        place,
        out_shape=(
            jax.ShapeDtypeStruct(master.shape, F32),
            jax.ShapeDtypeStruct((tokens, width), BF16),
        ),
        in_specs=[hbm] * 2,
        out_specs=(hbm, hbm),
        scratch_shapes=[dma((1 + 8 * K,))],
        compiler_params=pltpu.CompilerParams(vmem_limit_bytes=2**20),
        name="place",
    )(pltpu.with_memory_space_constraint(new_master, vm), pltpu.with_memory_space_constraint(mixed, vm))


def solution(mesh):
    in_specs = (
        P("dp", "tensor", None),
        P("tensor", "dp"),
        P("tensor", "dp"),
        P("tensor", "dp"),
        P("dp", "tensor"),
        P("dp", "tensor"),
    )
    out_specs = (P("tensor", "dp"), P("dp", None))
    return jax.shard_map(
        per_device, mesh=mesh, in_specs=in_specs, out_specs=out_specs, check_vma=False
    )
```

```python
import functools
import math

import jax
import jax.numpy as jnp
from jax import lax
from jax.experimental import pallas as pl
from jax.experimental.pallas import tpu as pltpu
from jax.sharding import PartitionSpec as P

FF = 14336

beta_one = 0.9
beta_two = 0.95
epsilon = 1e-08
weight_decay = 0.1
step_count = 20

MESH = pl.DeviceIdType.MESH
F32 = jnp.float32
BF16 = jnp.bfloat16

K = 4
LANES = 128
HP = 8


def sweep(rows, tile, body):
    if rows == tile:
        body(0)
        return

    @pl.loop(0, rows // tile)
    def _(i):
        body(pl.multiple_of(i * tile, tile))


def plan():
    return [
        ("X1", 0), ("R", 0), ("HID",), ("H", 7), ("H", 1), ("H", 3), ("X2", 0), ("X1", 1), ("X3", 0), ("H", 0),
        ("R", 1), ("X2", 1), ("Y1", 0), ("H", 4), ("X1", 2), ("X3", 1), ("H", 5), ("A2", 0), ("M", 0, 0, 0),
        ("Z0", 0, 0, 0), ("Y1", 1), ("R", 2), ("H", 2), ("H", 6), ("Z2", 0, 0, 0), ("M", 0, 0, 1),
        ("Z0", 0, 0, 1), ("A2", 1), ("X2", 2), ("M", 1, 0, 0), ("Z0", 1, 0, 0), ("Z3", 0, 0, 0),
        ("Z2", 0, 0, 1), ("X1", 3), ("R", 3), ("M", 0, 1, 1), ("M", 1, 1, 0), ("Z2", 1, 0, 0), ("Z0", 0, 1, 1),
        ("M", 1, 1, 1), ("Y2", 0, 0, 0), ("Z3", 0, 0, 1), ("Z0", 1, 1, 0), ("M", 0, 1, 0), ("Z3", 1, 0, 0),
        ("Z2", 0, 1, 1), ("Z0", 1, 1, 1), ("X3", 2), ("Z0", 0, 1, 0), ("M", 1, 0, 1), ("Z2", 1, 1, 0),
        ("Z2", 1, 1, 1), ("Z0", 1, 0, 1), ("Z3", 0, 1, 1), ("X2", 3), ("Z2", 0, 1, 0), ("Y2", 0, 0, 1),
        ("Z3", 1, 1, 1), ("Z2", 1, 0, 1), ("Z3", 1, 1, 0), ("Y2", 1, 0, 0), ("Y1", 2), ("Y2", 0, 1, 1),
        ("O2", 0, 0, 0), ("Z3", 0, 1, 0), ("Y2", 1, 1, 1), ("Z3", 1, 0, 1), ("Y2", 1, 1, 0), ("X3", 3),
        ("O2", 0, 1, 1), ("O2", 0, 0, 1), ("Y2", 0, 1, 0), ("Y2", 1, 0, 1), ("O2", 1, 1, 1), ("O2", 1, 0, 0),
        ("O2", 1, 1, 0), ("A2", 2), ("M", 2, 0, 0), ("M", 2, 1, 0), ("Z0", 2, 0, 0), ("Y1", 3), ("O2", 0, 1, 0),
        ("O2", 1, 0, 1), ("Z0", 2, 1, 0), ("M", 2, 1, 1), ("Z2", 2, 0, 0), ("M", 2, 0, 1), ("Z0", 2, 1, 1),
        ("Z0", 2, 0, 1), ("Z2", 2, 1, 0), ("Z3", 2, 0, 0), ("A2", 3), ("M", 3, 1, 0), ("Z2", 2, 1, 1),
        ("Z2", 2, 0, 1), ("M", 3, 0, 0), ("Z0", 3, 1, 0), ("O3", 1, 0, 1), ("Z3", 2, 1, 0), ("Z0", 3, 0, 0),
        ("Y2", 2, 0, 0), ("M", 3, 1, 1), ("E", 1, 0, 1), ("Z2", 3, 1, 0), ("M", 3, 0, 1), ("Z2", 3, 0, 0),
        ("Z0", 3, 1, 1), ("Z3", 2, 0, 1), ("Z0", 3, 0, 1), ("Z3", 2, 1, 1), ("O2", 2, 0, 0), ("O3", 0, 0, 0),
        ("O3", 1, 1, 1), ("O3", 1, 1, 0), ("Z3", 3, 1, 0), ("Z2", 3, 1, 1), ("Y2", 2, 1, 0), ("Z3", 3, 0, 0),
        ("Z2", 3, 0, 1), ("Y2", 2, 1, 1), ("O3", 1, 0, 0), ("Y2", 3, 1, 0), ("Z3", 3, 1, 1), ("Y2", 2, 0, 1),
        ("O3", 0, 1, 1), ("Z3", 3, 0, 1), ("Y2", 3, 0, 0), ("O2", 3, 1, 0), ("O3", 0, 0, 1), ("Y2", 3, 1, 1),
        ("O3", 0, 1, 0), ("E", 0, 0, 0), ("O2", 2, 0, 1), ("Y2", 3, 0, 1), ("E", 1, 1, 0), ("E", 1, 0, 0),
        ("O2", 3, 0, 0), ("O2", 2, 1, 0), ("O3", 2, 0, 0), ("O2", 3, 1, 1), ("O3", 2, 0, 1), ("O3", 3, 1, 0),
        ("E", 2, 0, 0), ("O2", 2, 1, 1), ("E", 0, 1, 1), ("O2", 3, 0, 1), ("O3", 3, 0, 0), ("E", 0, 0, 1),
        ("O3", 2, 1, 0), ("E", 3, 1, 0), ("O3", 3, 1, 1), ("O3", 2, 1, 1), ("E", 2, 0, 1), ("O3", 3, 0, 1),
        ("E", 2, 1, 1), ("E", 3, 1, 1), ("E", 1, 1, 1), ("E", 2, 1, 0), ("E", 3, 0, 0), ("E", 0, 1, 0),
        ("E", 3, 0, 1),
    ]


def kernel(
    g, mst, mom, sqr, gate, up,
    mst_v, out,
    gown, gfw, r1, r2, sy, ry, mom_v, sqr_v, w, gate_v, up_v, hid,
    p, rc, zr1, zr2, yb, yr,
    ld,
    x1s, x1r, rws, rwr, x2s, x2r, ys, yrs, a1s, a1r, a2s, a2r, hs, hr,
    cs, cr, z1s, z1r, zws, zwr, z2s, z2r, y3s, y3r, o1s, o1r, o2s, o2r, ocs, ocr,
):
    dp, t = lax.axis_index("dp"), lax.axis_index("tensor")
    x, yl = lax.div(dp, 2), lax.rem(dp, 2)
    z, yh, c = lax.div(t, 4), lax.rem(lax.div(t, 2), 2), lax.rem(t, 2)
    xn, xp = lax.rem(x + 1, 4), lax.rem(x + 3, 4)
    xo = lax.rem(x + 2, 4)
    zn, zp = lax.rem(z + 1, 4), lax.rem(z + 3, 4)
    zo = lax.rem(z + 2, 4)

    def dev(x=x, yl=yl, z=z, yh=yh, c=c):
        return (x * 2 + yl, z * 4 + yh * 2 + c)

    X = (dev(x=xn), dev(x=xp))
    Z = (dev(z=zn), dev(z=zp))
    YL = dev(yl=1 - yl)
    YH = dev(yh=1 - yh)
    YD = dev(yl=1 - yl, yh=1 - yh)
    C = dev(c=1 - c)

    rows = gown.shape[1]
    half = rows // 2
    tokens = hid.shape[1]
    core_rows = tokens // 2
    zrows = core_rows // 4
    zh = zrows // 2

    sends = []
    done = {}
    seen = set()

    def arrive(*keys):
        for key in keys:
            if key not in seen:
                seen.add(key)
                done[key].wait_recv()

    def remote(src, dst, s, r, to):
        cp = pltpu.make_async_remote_copy(
            src_ref=src, dst_ref=dst, send_sem=s, recv_sem=r, device_id=to, device_id_type=MESH
        )
        cp.start()
        sends.append(cp)
        return cp

    def columns(owner, strip, k, width=LANES):
        return pl.ds(pl.multiple_of(owner * (2 * K * LANES) + strip * (K * LANES) + k * LANES, LANES), width)

    loads = {}

    def load(name, i, src, dst):
        cp = pltpu.make_async_copy(src, dst, ld.at[i])
        cp.start()
        loads[name] = cp

    block = K * LANES
    load("f0", 0, g.at[0, :, columns(xn, 0, 0, block)], gfw.at[0])
    load("f1", 1, g.at[0, :, columns(xp, 1, 0, block)], gfw.at[1])
    load("gate", 2, gate, gate_v)
    load("up", 3, up, up_v)
    load("own0", 4, g.at[0, :, columns(x, 0, 0, block)], gown.at[0])
    load("own1", 5, g.at[0, :, columns(x, 1, 0, block)], gown.at[1])
    load("mst", 6, mst, mst_v)
    load("mom", 7, mom, mom_v)
    load("sqr", 8, sqr, sqr_v)

    def loaded(*names):
        for n in names:
            if n in loads:
                loads.pop(n).wait()

    barrier = pltpu.get_barrier_semaphore()
    friends = (*X, *Z, YL, YH, YD, C)
    for d in friends:
        pl.semaphore_signal(barrier, inc=1, device_id=d, device_id_type=MESH)
    pl.semaphore_wait(barrier, len(friends))

    def X1(k):
        done["x1", 0, k] = remote(
            g.at[0, :, columns(xo, 0, k)], r1.at[0, k], x1s.at[0, k], x1r.at[0, k], X[0])
        done["x1", 1, k] = remote(
            g.at[0, :, columns(xo, 1, k)], r1.at[1, k], x1s.at[1, k], x1r.at[1, k], X[1])

    def R(k):
        done["rw", 0, k] = remote(
            g.at[0, :, columns(xn, 1, k)], r2.at[0, k, 1], rws.at[0, k], rwr.at[0, k], X[0])
        done["rw", 1, k] = remote(
            g.at[0, :, columns(xp, 0, k)], r2.at[1, k, 0], rws.at[1, k], rwr.at[1, k], X[1])

    def X2(k):
        loaded("f0", "f1")
        cols = pl.ds(k * LANES, LANES)
        for d in (0, 1):
            done["x1", d, k].wait_recv()

            def body(r):
                at = pl.ds(r, 128)
                gfw[d, at, cols] = (gfw[d, at, cols].astype(F32) + r1[d, k, at, :].astype(F32)).astype(BF16)

            sweep(rows, 128, body)
            done["x2", d, k] = remote(
                gfw.at[d, :, cols], r2.at[d, k, d], x2s.at[d, k], x2r.at[d, k], X[d])

    def X3(k):
        loaded("own0", "own1")
        for d in (0, 1):
            done["rw", d, k].wait_recv()
            done["x2", d, k].wait_recv()
        cols = pl.ds(k * LANES, LANES)
        other = 1 - yl

        def body(r):
            at = pl.ds(r, 128)
            sy[k, at, :] = (
                gown[other, at, cols].astype(F32)
                + r2[0, k, other, at, :].astype(F32)
                + r2[1, k, other, at, :].astype(F32)
            ).astype(BF16)

        sweep(rows, 128, body)
        done["y", k] = remote(sy.at[k], ry.at[k], ys.at[k], yrs.at[k], YL)

    learn_rate = 0.8 / math.sqrt(FF)
    corr_one = 1.0 - beta_one**step_count
    corr_two = 1.0 - beta_two**step_count

    def Y1(k):
        loaded("mst", "mom", "sqr")
        done["y", k].wait_recv()
        cols = pl.ds(k * LANES, LANES)

        def body(r):
            at = pl.ds(r, 64)
            grad = (
                gown[yl, at, cols].astype(F32)
                + r2[0, k, yl, at, :].astype(F32)
                + r2[1, k, yl, at, :].astype(F32)
                + ry[k, at, :].astype(F32)
            )
            moment_new = beta_one * mom_v[at, cols] + (1.0 - beta_one) * grad
            square_new = beta_two * sqr_v[at, cols] + (1.0 - beta_two) * grad * grad
            update = moment_new / corr_one / (jnp.sqrt(square_new / corr_two) + epsilon)
            old = mst_v[at, cols]
            new = old - learn_rate * (update + weight_decay * old)
            mst_v[at, cols] = new
            w[k, 0, at, :] = new.astype(BF16)

        sweep(rows, 64, body)
        for d in (0, 1):
            done["a1", d, k] = remote(
                w.at[k, 0], w.at[k, 2 - d], a1s.at[d, k], a1r.at[d, k], X[d])

    def A2(k):
        for d in (0, 1):
            arrive(("a1", d, k))
            at = pl.ds(d * half, half)
            done["a2", d, k] = remote(
                w.at[k, 2 - d, at], w.at[k, 3, at], a2s.at[d, k], a2r.at[d, k], X[d])

    piece = tokens // HP

    def HID():
        loaded("gate", "up")

        def body(r):
            at = pl.ds(r, 32)
            v = gate_v[at, :].astype(F32)
            hid[0, at, :] = (v / (1.0 + jnp.exp(-v)) * up_v[at, :].astype(F32)).astype(BF16)

        sweep(tokens, 32, body)

    def H(i):
        at = pl.ds(i * piece, piece)
        done["h", i] = remote(hid.at[0, at], hid.at[1, at], hs.at[i], hr.at[i], YL)

    def M(k, h, q):
        arrive(("a1", 0, k), ("a1", 1, k))
        if q == 1:
            arrive(("a2", 0, k), ("a2", 1, k))
        if h == 1:
            arrive(*(("h", i) for i in range(HP)))
        for part in (1 - c, c):
            at = pl.ds(pl.multiple_of(part * core_rows, core_rows), core_rows)
            weights = jnp.concatenate([w[k, 2 * q], w[k, 2 * q + 1]], axis=1)
            p[k, h, q, at, :] = jnp.dot(
                hid[h, at, :], weights, preferred_element_type=F32).astype(BF16)
            if part is not c:
                done["c", k, h, q] = remote(p.at[k, h, q, at], rc.at[k, h, q], cs.at[k, h, q], cr.at[k, h, q], C)

    base = c * core_rows

    def zat(owner, part, count):
        return pl.ds(pl.multiple_of(base + owner * zrows + part * zh, zh), count)

    def Z0(k, h, q):
        arrive(("c", k, h, q))

        def body(r):
            at = pl.ds(pl.multiple_of(base + r, 128), 128)
            p[k, h, q, at, :] = (
                p[k, h, q, at, :].astype(F32) + rc[k, h, q, pl.ds(r, 128), :].astype(F32)).astype(BF16)

        sweep(core_rows, 128, body)
        for d in (0, 1):
            done["z1", d, k, h, q] = remote(
                p.at[k, h, q, zat(zo, d, zh)], zr1.at[d, k, h, q], z1s.at[d, k, h, q], z1r.at[d, k, h, q], Z[d])
        for d, owner in ((0, zn), (1, zp)):
            done["zw", d, k, h, q] = remote(
                p.at[k, h, q, zat(owner, 1 - d, zh)], zr2.at[d, k, h, q, pl.ds((1 - d) * zh, zh)],
                zws.at[d, k, h, q], zwr.at[d, k, h, q], Z[d])

    def Z2(k, h, q):
        for d, owner in ((0, zn), (1, zp)):
            arrive(("z1", d, k, h, q))
            at = zat(owner, d, zh)
            p[k, h, q, at, :] = (p[k, h, q, at, :].astype(F32) + zr1[d, k, h, q].astype(F32)).astype(BF16)
            done["z2", d, k, h, q] = remote(
                p.at[k, h, q, at], zr2.at[d, k, h, q, pl.ds(d * zh, zh)], z2s.at[d, k, h, q], z2r.at[d, k, h, q], Z[d])

    def Z3(k, h, q):
        for d in (0, 1):
            arrive(("zw", d, k, h, q), ("z2", d, k, h, q))
        for part in (0, 1):
            at = pl.ds(part * zh, zh)
            yb[k, h, q, at, :] = (
                p[k, h, q, zat(z, part, zh), :].astype(F32)
                + zr2[0, k, h, q, at, :].astype(F32)
                + zr2[1, k, h, q, at, :].astype(F32)
            ).astype(BF16)
        for i, to in ((0, YH),) if h == 0 else ((1, YL), (2, YD)):
            done["y3", i, k, q] = remote(yb.at[k, h, q], yr.at[i, k, q], y3s.at[i, k, q], y3r.at[i, k, q], to)

    def Y2(k, h, q):
        group = yl if h == 0 else 1 - yl
        arrive(*(("y3", i, k, q) for i in ((0,) if h == 0 else (1, 2))))
        for part in (0, 1):
            at = pl.ds(part * zh, zh)
            if h == 0:
                total = yb[k, 0, q, at, :].astype(F32) + yr[0, k, q, at, :].astype(F32)
            else:
                total = yr[1, k, q, at, :].astype(F32) + yr[2, k, q, at, :].astype(F32)
            out[k, group, q, zat(z, part, zh), :] = total.astype(BF16)
        mine = out.at[k, group, q, zat(z, 0, zrows)]
        for d in (0, 1):
            done["o1", d, k, h, q] = remote(mine, mine, o1s.at[d, k, h, q], o1r.at[d, k, h, q], Z[d])

    def O2(k, h, q):
        group = yl if h == 0 else 1 - yl
        for d, origin in ((0, zp), (1, zn)):
            arrive(("o1", d, k, h, q))
            part = out.at[k, group, q, zat(origin, d, zh)]
            done["o2", d, k, h, q] = remote(part, part, o2s.at[d, k, h, q], o2r.at[d, k, h, q], Z[d])

    def O3(k, h, q):
        group = yl if h == 0 else 1 - yl
        arrive(("o2", 0, k, h, q), ("o2", 1, k, h, q))
        part = out.at[k, group, q, pl.ds(pl.multiple_of(base, core_rows), core_rows)]
        done["oc", k, h, q] = remote(part, part, ocs.at[k, h, q], ocr.at[k, h, q], C)

    def E(k, h, q):
        arrive(("oc", k, h, q))

    steps = dict(X1=X1, R=R, X2=X2, X3=X3, Y1=Y1, A2=A2, HID=HID, H=H, M=M, Z0=Z0, Z2=Z2, Z3=Z3, Y2=Y2, O2=O2, O3=O3, E=E)
    for name, *at in plan():
        steps[name](*at)

    for cp in sends:
        cp.wait_send()


def place(nm, out, nm_out, mix_out, sems):
    x = lax.div(lax.axis_index("dp"), 2)
    copies = [pltpu.make_async_copy(nm, nm_out, sems.at[0])]
    for k in range(K):
        for group in (0, 1):
            for slot, ahead in enumerate((0, 1, 3, 2)):
                owner = lax.rem(x + ahead, 4)
                at = pl.ds(pl.multiple_of((owner * 2 * K + group * K + k) * LANES, LANES), LANES)
                copies.append(pltpu.make_async_copy(
                    out.at[k, group, slot // 2, :, pl.ds(slot % 2 * LANES, LANES)],
                    mix_out.at[:, at], sems.at[len(copies)]))
    for cp in copies:
        cp.start()
    for cp in copies:
        cp.wait()


def per_device(grad_parts, master, moment_one, moment_two, gate_act, up_act):
    _, rows, width = grad_parts.shape
    tokens = gate_act.shape[0]
    hbm = pl.BlockSpec(memory_space=pl.ANY)
    block = K * LANES
    vm = pltpu.VMEM
    dma = pltpu.SemaphoreType.DMA

    def pair(shape):
        return [dma(shape), dma(shape)]

    new_master, mixed = pl.pallas_call(
        kernel,
        out_shape=(
            vm(master.shape, F32),
            vm((K, 2, 2, tokens, block // 2), BF16),
        ),
        in_specs=[hbm] * 6,
        scratch_shapes=[
            vm((2, rows, block), BF16),
            vm((2, rows, block), BF16),
            vm((2, K, rows, LANES), BF16),
            vm((2, K, 2, rows, LANES), BF16),
            vm((K, rows, LANES), BF16),
            vm((K, rows, LANES), BF16),
            vm((rows, block), F32),
            vm((rows, block), F32),
            vm((K, 4, rows, LANES), BF16),
            vm((tokens, rows), BF16),
            vm((tokens, rows), BF16),
            vm((2, tokens, rows), BF16),
            vm((K, 2, 2, tokens, block // 2), BF16),
            vm((K, 2, 2, tokens // 2, block // 2), BF16),
            vm((2, K, 2, 2, tokens // 16, block // 2), BF16),
            vm((2, K, 2, 2, tokens // 8, block // 2), BF16),
            vm((K, 2, 2, tokens // 8, block // 2), BF16),
            vm((3, K, 2, tokens // 8, block // 2), BF16),
            dma((9,)),
            *pair((2, K)), *pair((2, K)), *pair((2, K)), *pair((K,)),
            *pair((2, K)), *pair((2, K)), *pair((HP,)),
            *pair((K, 2, 2)), *pair((2, K, 2, 2)), *pair((2, K, 2, 2)), *pair((2, K, 2, 2)),
            *pair((3, K, 2)), *pair((2, K, 2, 2)), *pair((2, K, 2, 2)), *pair((K, 2, 2)),
        ],
        compiler_params=pltpu.CompilerParams(
            collective_id=0, has_side_effects=True, vmem_limit_bytes=50 * 2**20
        ),
        name="handover",
    )(grad_parts, master, moment_one, moment_two, gate_act, up_act)
    return pl.pallas_call(
        place,
        out_shape=(
            jax.ShapeDtypeStruct(master.shape, F32),
            jax.ShapeDtypeStruct((tokens, width), BF16),
        ),
        in_specs=[hbm] * 2,
        out_specs=(hbm, hbm),
        scratch_shapes=[dma((1 + 8 * K,))],
        compiler_params=pltpu.CompilerParams(vmem_limit_bytes=2**20),
        name="place",
    )(pltpu.with_memory_space_constraint(new_master, vm), pltpu.with_memory_space_constraint(mixed, vm))


def solution(mesh):
    in_specs = (
        P("dp", "tensor", None),
        P("tensor", "dp"),
        P("tensor", "dp"),
        P("tensor", "dp"),
        P("dp", "tensor"),
        P("dp", "tensor"),
    )
    out_specs = (P("tensor", "dp"), P("dp", None))
    return jax.shard_map(
        per_device, mesh=mesh, in_specs=in_specs, out_specs=out_specs, check_vma=False
    )
```

```python
import functools
import math

import jax
import jax.numpy as jnp
from jax import lax
from jax.experimental import pallas as pl
from jax.experimental.pallas import tpu as pltpu
from jax.sharding import PartitionSpec as P

FF = 14336

beta_one = 0.9
beta_two = 0.95
epsilon = 1e-08
weight_decay = 0.1
step_count = 20

MESH = pl.DeviceIdType.MESH
F32 = jnp.float32
BF16 = jnp.bfloat16

K = 4
LANES = 128
HP = 8
LATER = 6


def sweep(rows, tile, body):
    if rows == tile:
        body(0)
        return

    @pl.loop(0, rows // tile)
    def _(i):
        body(pl.multiple_of(i * tile, tile))


def plan():
    return [
        ("X1", 1), ("HID", 6), ("H", 6), ("HID", 4), ("HID", 2), ("L", 1), ("H", 4), ("HID", 3), ("R", 1),
        ("L", 0), ("X1", 2), ("X2", 1, 0), ("H", 3), ("HID", 1), ("L", 2), ("X2", 1, 1), ("HID", 5), ("R", 2),
        ("H", 2), ("HID", 7), ("X3", 1, 0), ("X2", 2, 0), ("X2", 2, 1), ("X3", 1, 1), ("H", 7), ("Y1", 1, 1),
        ("X3", 2, 0), ("HID", 0), ("Y1", 1, 0), ("X1", 0), ("X3", 2, 1), ("H", 0), ("M", 1, 0, 0), ("A2", 1, 0),
        ("A2", 1, 1), ("H", 1), ("Y1", 2, 0), ("Y1", 2, 1), ("Z0", 1, 0, 0), ("R", 0), ("H", 5), ("X2", 0, 0),
        ("Z2", 1, 0, 0), ("M", 1, 0, 1), ("X2", 0, 1), ("Z3", 1, 0, 0), ("Z0", 1, 0, 1), ("A2", 2, 0),
        ("M", 2, 0, 0), ("Z2", 1, 0, 1), ("A2", 2, 1), ("X1", 3), ("Z0", 2, 0, 0), ("M", 1, 1, 1),
        ("Z3", 1, 0, 1), ("Y2", 1, 0, 0), ("M", 2, 1, 0), ("Z2", 2, 0, 0), ("Z0", 1, 1, 1), ("X3", 0, 0),
        ("Z0", 2, 1, 0), ("M", 1, 1, 0), ("X3", 0, 1), ("Y2", 1, 0, 1), ("Z3", 2, 0, 0), ("Z0", 1, 1, 0),
        ("Z2", 1, 1, 1), ("O2", 1, 0, 0), ("Z2", 2, 1, 0), ("M", 2, 0, 1), ("Y1", 0, 0), ("O2", 1, 0, 1),
        ("M", 2, 1, 1), ("Z2", 1, 1, 0), ("Y1", 0, 1), ("Z0", 2, 0, 1), ("O3", 1, 0, 0), ("Z3", 1, 1, 1),
        ("R", 3), ("Z0", 2, 1, 1), ("X2", 3, 1), ("Z3", 2, 1, 0), ("Y2", 2, 0, 0), ("Z3", 1, 1, 0),
        ("X2", 3, 0), ("Z2", 2, 0, 1), ("Y2", 1, 1, 1), ("A2", 0, 1), ("Z2", 2, 1, 1), ("M", 0, 0, 0),
        ("Y2", 2, 1, 0), ("M", 0, 1, 0), ("Z0", 0, 0, 0), ("Z3", 2, 0, 1), ("A2", 0, 0), ("Z0", 0, 1, 0),
        ("Z3", 2, 1, 1), ("Y2", 1, 1, 0), ("Z2", 0, 0, 0), ("X3", 3, 1), ("Z2", 0, 1, 0), ("Y2", 2, 0, 1),
        ("Y2", 2, 1, 1), ("O2", 1, 1, 1), ("X3", 3, 0), ("Z3", 0, 0, 0), ("O2", 2, 1, 0), ("O2", 2, 0, 0),
        ("Z3", 0, 1, 0), ("O2", 1, 1, 0), ("Y1", 3, 1), ("M", 0, 0, 1), ("O2", 2, 1, 1), ("O2", 2, 0, 1),
        ("Y1", 3, 0), ("Z0", 0, 0, 1), ("M", 0, 1, 1), ("Y2", 0, 0, 0), ("Y2", 0, 1, 0), ("A2", 3, 1),
        ("Z0", 0, 1, 1), ("Z2", 0, 0, 1), ("O3", 2, 0, 0), ("A2", 3, 0), ("M", 3, 0, 0), ("O2", 0, 0, 0),
        ("M", 3, 1, 0), ("Z0", 3, 0, 0), ("O2", 0, 1, 0), ("Z2", 0, 1, 1), ("Z0", 3, 1, 0), ("Z3", 0, 0, 1),
        ("M", 3, 0, 1), ("Z2", 3, 0, 0), ("M", 3, 1, 1), ("Z0", 3, 0, 1), ("O3", 1, 1, 0), ("E", 2, 0, 0),
        ("O3", 2, 1, 1), ("Z3", 0, 1, 1), ("Z2", 3, 1, 0), ("Z0", 3, 1, 1), ("Z3", 3, 0, 0), ("Z2", 3, 0, 1),
        ("Y2", 0, 0, 1), ("Z3", 3, 1, 0), ("E", 1, 0, 0), ("Z2", 3, 1, 1), ("Y2", 0, 1, 1), ("Z3", 3, 0, 1),
        ("E", 2, 1, 1), ("O3", 2, 1, 0), ("Y2", 3, 0, 0), ("Z3", 3, 1, 1), ("O3", 1, 0, 1), ("Y2", 3, 1, 0),
        ("O2", 0, 1, 1), ("E", 1, 0, 1), ("Y2", 3, 0, 1), ("O3", 0, 1, 0), ("O3", 1, 1, 1), ("Y2", 3, 1, 1),
        ("O2", 0, 0, 1), ("O2", 3, 0, 0), ("O3", 0, 0, 0), ("E", 2, 1, 0), ("O2", 3, 1, 0), ("O3", 0, 1, 1),
        ("O2", 3, 0, 1), ("O2", 3, 1, 1), ("O3", 2, 0, 1), ("O3", 0, 0, 1), ("E", 0, 1, 1), ("O3", 3, 0, 0),
        ("E", 1, 1, 0), ("O3", 3, 1, 0), ("E", 2, 0, 1), ("E", 0, 0, 0), ("E", 0, 1, 0), ("O3", 3, 0, 1),
        ("O3", 3, 1, 1), ("E", 0, 0, 1), ("E", 3, 1, 0), ("E", 3, 0, 0), ("E", 1, 1, 1), ("E", 3, 0, 1),
        ("E", 3, 1, 1),
    ]


def kernel(
    g, mst, mom, sqr, gate, up,
    mst_v, out,
    gv, r1, r2, sy, ry, mom_v, sqr_v, w, gate_v, up_v, hid,
    p, rc, zr1, zr2, yb, yr,
    lg, ld,
    x1s, x1r, rws, rwr, x2s, x2r, ys, yrs, a1s, a1r, a2s, a2r, hs, hr,
    cs, cr, z1s, z1r, zws, zwr, z2s, z2r, y3s, y3r, o1s, o1r, o2s, o2r, ocs, ocr,
):
    dp, t = lax.axis_index("dp"), lax.axis_index("tensor")
    x, yl = lax.div(dp, 2), lax.rem(dp, 2)
    z, yh, c = lax.div(t, 4), lax.rem(lax.div(t, 2), 2), lax.rem(t, 2)
    xn, xp = lax.rem(x + 1, 4), lax.rem(x + 3, 4)
    xo = lax.rem(x + 2, 4)
    zn, zp = lax.rem(z + 1, 4), lax.rem(z + 3, 4)
    zo = lax.rem(z + 2, 4)

    def dev(x=x, yl=yl, z=z, yh=yh, c=c):
        return (x * 2 + yl, z * 4 + yh * 2 + c)

    X = (dev(x=xn), dev(x=xp))
    Z = (dev(z=zn), dev(z=zp))
    YL = dev(yl=1 - yl)
    YH = dev(yh=1 - yh)
    YD = dev(yl=1 - yl, yh=1 - yh)
    C = dev(c=1 - c)

    rows = gv.shape[3]
    half = rows // 2
    tokens = hid.shape[1]
    core_rows = tokens // 2
    zrows = core_rows // 4
    zh = zrows // 2

    done = {}
    seen = set()
    settled = []
    step_at = [0]

    def arrive(*keys):
        for key in keys:
            if key not in seen:
                seen.add(key)
                done[key].wait_recv()
                settled.append((step_at[0], done[key]))

    def remote(src, dst, s, r, to):
        cp = pltpu.make_async_remote_copy(
            src_ref=src, dst_ref=dst, send_sem=s, recv_sem=r, device_id=to, device_id_type=MESH
        )
        cp.start()
        return cp

    def columns(owner, strip, k, width=LANES):
        return pl.ds(pl.multiple_of(owner * (2 * K * LANES) + strip * (K * LANES) + k * LANES, LANES), width)

    loads = {}
    ready = set()

    def load(name, sem, src, dst):
        cp = pltpu.make_async_copy(src, dst, sem)
        cp.start()
        loads[name] = cp

    def loaded(*names):
        for n in names:
            if n not in ready:
                ready.add(n)
                loads.pop(n).wait()

    owners = (x, xn, xo, xp)

    def loadg(k):
        for o, strip in ((2, 0), (2, 1), (1, 1), (3, 0), (1, 0), (3, 1), (0, 0), (0, 1)):
            load(("g", o, strip, k), lg.at[o, strip, k], g.at[0, :, columns(owners[o], strip, k)], gv.at[o, strip, k])

    chunks = [step[1] for step in plan() if step[0] == "X1"]
    loadg(chunks[0])
    load("gate", ld.at[0], gate, gate_v)
    load("up", ld.at[1], up, up_v)

    def L(i):
        if i == 0:
            loadg(chunks[1])
        elif i == 1:
            loadg(chunks[2])
            loadg(chunks[3])
        else:
            load("mst", ld.at[2], mst, mst_v)
            load("mom", ld.at[3], mom, mom_v)
            load("sqr", ld.at[4], sqr, sqr_v)

    barrier = pltpu.get_barrier_semaphore()
    friends = (*X, *Z, YL, YH, YD, C)
    for d in friends:
        pl.semaphore_signal(barrier, inc=1, device_id=d, device_id_type=MESH)
    pl.semaphore_wait(barrier, len(friends))

    def X1(k):
        for d in (0, 1):
            loaded(("g", 2, d, k))
            done["x1", d, k] = remote(gv.at[2, d, k], r1.at[d, k], x1s.at[d, k], x1r.at[d, k], X[d])

    def R(k):
        for d, o in ((0, 1), (1, 3)):
            loaded(("g", o, 1 - d, k))
            done["rw", d, k] = remote(
                gv.at[o, 1 - d, k], r2.at[d, k, 1 - d], rws.at[d, k], rwr.at[d, k], X[d])

    def X2(k, part):
        at_part = pl.ds(part * half, half)
        for d, o in ((0, 1), (1, 3)):
            loaded(("g", o, d, k))
            arrive(("x1", d, k))

            def body(r):
                at = pl.ds(pl.multiple_of(part * half + r, 64), 64)
                gv[o, d, k, at, :] = (gv[o, d, k, at, :].astype(F32) + r1[d, k, at, :].astype(F32)).astype(BF16)

            sweep(half, 64, body)
            done["x2", d, k, part] = remote(
                gv.at[o, d, k, at_part], r2.at[d, k, d, at_part], x2s.at[d, k, part], x2r.at[d, k, part], X[d])

    def X3(k, part):
        loaded(("g", 0, 0, k), ("g", 0, 1, k))
        for d in (0, 1):
            arrive(("rw", d, k), ("x2", d, k, part))
        other = 1 - yl

        def body(r):
            at = pl.ds(pl.multiple_of(part * half + r, 64), 64)
            sy[k, at, :] = (
                gv[0, other, k, at, :].astype(F32)
                + r2[0, k, other, at, :].astype(F32)
                + r2[1, k, other, at, :].astype(F32)
            ).astype(BF16)

        sweep(half, 64, body)
        at_part = pl.ds(part * half, half)
        done["y", k, part] = remote(sy.at[k, at_part], ry.at[k, at_part], ys.at[k, part], yrs.at[k, part], YL)

    learn_rate = 0.8 / math.sqrt(FF)
    corr_one = 1.0 - beta_one**step_count
    corr_two = 1.0 - beta_two**step_count

    def Y1(k, part):
        loaded("mst", "mom", "sqr")
        arrive(("y", k, part))
        cols = pl.ds(k * LANES, LANES)

        def body(r):
            at = pl.ds(pl.multiple_of(part * half + r, 64), 64)
            grad = (
                gv[0, yl, k, at, :].astype(F32)
                + r2[0, k, yl, at, :].astype(F32)
                + r2[1, k, yl, at, :].astype(F32)
                + ry[k, at, :].astype(F32)
            )
            moment_new = beta_one * mom_v[at, cols] + (1.0 - beta_one) * grad
            square_new = beta_two * sqr_v[at, cols] + (1.0 - beta_two) * grad * grad
            update = moment_new / corr_one / (jnp.sqrt(square_new / corr_two) + epsilon)
            old = mst_v[at, cols]
            new = old - learn_rate * (update + weight_decay * old)
            mst_v[at, cols] = new
            w[k, 0, at, :] = new.astype(BF16)

        sweep(half, 64, body)
        at_part = pl.ds(part * half, half)
        for d in (0, 1):
            done["a1", d, k, part] = remote(
                w.at[k, 0, at_part], w.at[k, 2 - d, at_part], a1s.at[d, k, part], a1r.at[d, k, part], X[d])

    def A2(k, d):
        arrive(("a1", d, k, d))
        at = pl.ds(d * half, half)
        done["a2", d, k] = remote(
            w.at[k, 2 - d, at], w.at[k, 3, at], a2s.at[d, k], a2r.at[d, k], X[d])

    piece = tokens // HP

    def HID(i):
        loaded("gate", "up")

        def body(r):
            at = pl.ds(pl.multiple_of(i * piece + r, 32), 32)
            v = gate_v[at, :].astype(F32)
            hid[0, at, :] = (v / (1.0 + jnp.exp(-v)) * up_v[at, :].astype(F32)).astype(BF16)

        sweep(piece, 32, body)

    def H(i):
        at = pl.ds(i * piece, piece)
        done["h", i] = remote(hid.at[0, at], hid.at[1, at], hs.at[i], hr.at[i], YL)

    def M(k, h, q):
        arrive(*(("a1", d, k, part) for d in (0, 1) for part in (0, 1)))
        if q == 1:
            arrive(("a2", 0, k), ("a2", 1, k))
        if h == 1:
            arrive(*(("h", i) for i in range(HP)))
        for part in (1 - c, c):
            at = pl.ds(pl.multiple_of(part * core_rows, core_rows), core_rows)
            weights = jnp.concatenate([w[k, 2 * q], w[k, 2 * q + 1]], axis=1)
            p[k, h, q, at, :] = jnp.dot(
                hid[h, at, :], weights, preferred_element_type=F32).astype(BF16)
            if part is not c:
                done["c", k, h, q] = remote(p.at[k, h, q, at], rc.at[k, h, q], cs.at[k, h, q], cr.at[k, h, q], C)

    base = c * core_rows

    def zat(owner, part, count):
        return pl.ds(pl.multiple_of(base + owner * zrows + part * zh, zh), count)

    def Z0(k, h, q):
        arrive(("c", k, h, q))

        def body(r):
            at = pl.ds(pl.multiple_of(base + r, 128), 128)
            p[k, h, q, at, :] = (
                p[k, h, q, at, :].astype(F32) + rc[k, h, q, pl.ds(r, 128), :].astype(F32)).astype(BF16)

        sweep(core_rows, 128, body)
        for d in (0, 1):
            done["z1", d, k, h, q] = remote(
                p.at[k, h, q, zat(zo, d, zh)], zr1.at[d, k, h, q], z1s.at[d, k, h, q], z1r.at[d, k, h, q], Z[d])
        for d, owner in ((0, zn), (1, zp)):
            done["zw", d, k, h, q] = remote(
                p.at[k, h, q, zat(owner, 1 - d, zh)], zr2.at[d, k, h, q, pl.ds((1 - d) * zh, zh)],
                zws.at[d, k, h, q], zwr.at[d, k, h, q], Z[d])

    def Z2(k, h, q):
        for d, owner in ((0, zn), (1, zp)):
            arrive(("z1", d, k, h, q))
            at = zat(owner, d, zh)
            p[k, h, q, at, :] = (p[k, h, q, at, :].astype(F32) + zr1[d, k, h, q].astype(F32)).astype(BF16)
            done["z2", d, k, h, q] = remote(
                p.at[k, h, q, at], zr2.at[d, k, h, q, pl.ds(d * zh, zh)], z2s.at[d, k, h, q], z2r.at[d, k, h, q], Z[d])

    def Z3(k, h, q):
        for d in (0, 1):
            arrive(("zw", d, k, h, q), ("z2", d, k, h, q))
        for part in (0, 1):
            at = pl.ds(part * zh, zh)
            yb[k, h, q, at, :] = (
                p[k, h, q, zat(z, part, zh), :].astype(F32)
                + zr2[0, k, h, q, at, :].astype(F32)
                + zr2[1, k, h, q, at, :].astype(F32)
            ).astype(BF16)
        for i, to in ((0, YH),) if h == 0 else ((1, YL), (2, YD)):
            done["y3", i, k, q] = remote(yb.at[k, h, q], yr.at[i, k, q], y3s.at[i, k, q], y3r.at[i, k, q], to)

    def Y2(k, h, q):
        group = yl if h == 0 else 1 - yl
        arrive(*(("y3", i, k, q) for i in ((0,) if h == 0 else (1, 2))))
        for part in (0, 1):
            at = pl.ds(part * zh, zh)
            if h == 0:
                total = yb[k, 0, q, at, :].astype(F32) + yr[0, k, q, at, :].astype(F32)
            else:
                total = yr[1, k, q, at, :].astype(F32) + yr[2, k, q, at, :].astype(F32)
            out[k, group, q, zat(z, part, zh), :] = total.astype(BF16)
        mine = out.at[k, group, q, zat(z, 0, zrows)]
        for d in (0, 1):
            done["o1", d, k, h, q] = remote(mine, mine, o1s.at[d, k, h, q], o1r.at[d, k, h, q], Z[d])

    def O2(k, h, q):
        group = yl if h == 0 else 1 - yl
        for d, origin in ((0, zp), (1, zn)):
            arrive(("o1", d, k, h, q))
            part = out.at[k, group, q, zat(origin, d, zh)]
            done["o2", d, k, h, q] = remote(part, part, o2s.at[d, k, h, q], o2r.at[d, k, h, q], Z[d])

    def O3(k, h, q):
        group = yl if h == 0 else 1 - yl
        arrive(("o2", 0, k, h, q), ("o2", 1, k, h, q))
        part = out.at[k, group, q, pl.ds(pl.multiple_of(base, core_rows), core_rows)]
        done["oc", k, h, q] = remote(part, part, ocs.at[k, h, q], ocr.at[k, h, q], C)

    def E(k, h, q):
        arrive(("oc", k, h, q))

    steps = dict(L=L, X1=X1, R=R, X2=X2, X3=X3, Y1=Y1, A2=A2, HID=HID, H=H, M=M, Z0=Z0, Z2=Z2, Z3=Z3, Y2=Y2, O2=O2, O3=O3, E=E)
    for number, (name, *at) in enumerate(plan()):
        step_at[0] = number
        steps[name](*at)
        while settled and settled[0][0] <= number - LATER:
            settled.pop(0)[1].wait_send()

    for _, cp in settled:
        cp.wait_send()


def place(nm, out, nm_out, mix_out, sems):
    x = lax.div(lax.axis_index("dp"), 2)
    copies = [pltpu.make_async_copy(nm, nm_out, sems.at[0])]
    for k in range(K):
        for group in (0, 1):
            for slot, ahead in enumerate((0, 1, 3, 2)):
                owner = lax.rem(x + ahead, 4)
                at = pl.ds(pl.multiple_of((owner * 2 * K + group * K + k) * LANES, LANES), LANES)
                copies.append(pltpu.make_async_copy(
                    out.at[k, group, slot // 2, :, pl.ds(slot % 2 * LANES, LANES)],
                    mix_out.at[:, at], sems.at[len(copies)]))
    for cp in copies:
        cp.start()
    for cp in copies:
        cp.wait()


def per_device(grad_parts, master, moment_one, moment_two, gate_act, up_act):
    _, rows, width = grad_parts.shape
    tokens = gate_act.shape[0]
    hbm = pl.BlockSpec(memory_space=pl.ANY)
    block = K * LANES
    vm = pltpu.VMEM
    dma = pltpu.SemaphoreType.DMA

    def pair(shape):
        return [dma(shape), dma(shape)]

    new_master, mixed = pl.pallas_call(
        kernel,
        out_shape=(
            vm(master.shape, F32),
            vm((K, 2, 2, tokens, block // 2), BF16),
        ),
        in_specs=[hbm] * 6,
        scratch_shapes=[
            vm((4, 2, K, rows, LANES), BF16),
            vm((2, K, rows, LANES), BF16),
            vm((2, K, 2, rows, LANES), BF16),
            vm((K, rows, LANES), BF16),
            vm((K, rows, LANES), BF16),
            vm((rows, block), F32),
            vm((rows, block), F32),
            vm((K, 4, rows, LANES), BF16),
            vm((tokens, rows), BF16),
            vm((tokens, rows), BF16),
            vm((2, tokens, rows), BF16),
            vm((K, 2, 2, tokens, block // 2), BF16),
            vm((K, 2, 2, tokens // 2, block // 2), BF16),
            vm((2, K, 2, 2, tokens // 16, block // 2), BF16),
            vm((2, K, 2, 2, tokens // 8, block // 2), BF16),
            vm((K, 2, 2, tokens // 8, block // 2), BF16),
            vm((3, K, 2, tokens // 8, block // 2), BF16),
            dma((4, 2, K)), dma((5,)),
            *pair((2, K)), *pair((2, K)), *pair((2, K, 2)), *pair((K, 2)),
            *pair((2, K, 2)), *pair((2, K)), *pair((HP,)),
            *pair((K, 2, 2)), *pair((2, K, 2, 2)), *pair((2, K, 2, 2)), *pair((2, K, 2, 2)),
            *pair((3, K, 2)), *pair((2, K, 2, 2)), *pair((2, K, 2, 2)), *pair((K, 2, 2)),
        ],
        compiler_params=pltpu.CompilerParams(
            collective_id=0, has_side_effects=True, vmem_limit_bytes=50 * 2**20
        ),
        name="handover",
    )(grad_parts, master, moment_one, moment_two, gate_act, up_act)
    return pl.pallas_call(
        place,
        out_shape=(
            jax.ShapeDtypeStruct(master.shape, F32),
            jax.ShapeDtypeStruct((tokens, width), BF16),
        ),
        in_specs=[hbm] * 2,
        out_specs=(hbm, hbm),
        scratch_shapes=[dma((1 + 8 * K,))],
        compiler_params=pltpu.CompilerParams(vmem_limit_bytes=2**20),
        name="place",
    )(pltpu.with_memory_space_constraint(new_master, vm), pltpu.with_memory_space_constraint(mixed, vm))


def solution(mesh):
    in_specs = (
        P("dp", "tensor", None),
        P("tensor", "dp"),
        P("tensor", "dp"),
        P("tensor", "dp"),
        P("dp", "tensor"),
        P("dp", "tensor"),
    )
    out_specs = (P("tensor", "dp"), P("dp", None))
    return jax.shard_map(
        per_device, mesh=mesh, in_specs=in_specs, out_specs=out_specs, check_vma=False
    )
```

```python
import functools
import math

import jax
import jax.numpy as jnp
from jax import lax
from jax.experimental import pallas as pl
from jax.experimental.pallas import tpu as pltpu
from jax.sharding import PartitionSpec as P

FF = 14336

beta_one = 0.9
beta_two = 0.95
epsilon = 1e-08
weight_decay = 0.1
step_count = 20

MESH = pl.DeviceIdType.MESH
F32 = jnp.float32
BF16 = jnp.bfloat16

K = 4
LANES = 128
HP = 8
LATER = 6


def sweep(rows, tile, body):
    if rows == tile:
        body(0)
        return

    @pl.loop(0, rows // tile)
    def _(i):
        body(pl.multiple_of(i * tile, tile))


def plan():
    return [
        ("X1", 1), ("HID", 2), ("H", 2), ("HID", 6), ("HID", 3), ("L", 1), ("HID", 7), ("HID", 1), ("L", 2),
        ("H", 1), ("R", 1), ("L", 0), ("HID", 4), ("X2", 1, 0), ("X2", 1, 1), ("X1", 3), ("R", 3), ("H", 4),
        ("X3", 1, 0), ("HID", 0), ("X3", 1, 1), ("HID", 5), ("H", 7), ("Y1", 1, 0), ("H", 0), ("X2", 3, 1),
        ("X2", 3, 0), ("H", 5), ("Y1", 1, 1), ("A2", 1, 0), ("X1", 0), ("X3", 3, 1), ("X3", 3, 0),
        ("M", 1, 0, 0), ("A2", 1, 1), ("H", 3), ("H", 6), ("Z0", 1, 0, 0), ("Y1", 3, 1), ("Y1", 3, 0),
        ("Z2", 1, 0, 0), ("M", 1, 0, 1), ("R", 0), ("Z0", 1, 0, 1), ("X2", 0, 1), ("X2", 0, 0), ("A2", 3, 1),
        ("Z3", 1, 0, 0), ("M", 3, 0, 0), ("Z2", 1, 0, 1), ("Z0", 3, 0, 0), ("M", 1, 1, 1), ("A2", 3, 0),
        ("Y2", 1, 0, 0), ("M", 3, 1, 0), ("Z2", 3, 0, 0), ("Z3", 1, 0, 1), ("X1", 2), ("Z0", 1, 1, 1),
        ("X3", 0, 1), ("Z0", 3, 1, 0), ("M", 1, 1, 0), ("X3", 0, 0), ("Z2", 1, 1, 1), ("Z0", 1, 1, 0),
        ("Y2", 1, 0, 1), ("Z3", 3, 0, 0), ("M", 3, 0, 1), ("Z2", 3, 1, 0), ("Y1", 0, 1), ("Z2", 1, 1, 0),
        ("Z3", 1, 1, 1), ("O2", 1, 0, 0), ("Z0", 3, 0, 1), ("Y1", 0, 0), ("M", 3, 1, 1), ("Y2", 3, 0, 0),
        ("Z3", 3, 1, 0), ("X2", 2, 1), ("R", 2), ("Z3", 1, 1, 0), ("Z0", 3, 1, 1), ("O2", 1, 0, 1),
        ("Z2", 3, 0, 1), ("O3", 1, 0, 0), ("Y2", 1, 1, 1), ("X2", 2, 0), ("Z2", 3, 1, 1), ("M", 0, 0, 0),
        ("Y2", 1, 1, 0), ("Y2", 3, 1, 0), ("Z3", 3, 0, 1), ("M", 0, 1, 0), ("Z0", 0, 0, 0), ("O2", 3, 0, 0),
        ("Z3", 3, 1, 1), ("A2", 0, 0), ("Z0", 0, 1, 0), ("A2", 0, 1), ("X3", 2, 1), ("Z2", 0, 0, 0),
        ("Y2", 3, 1, 1), ("Y2", 3, 0, 1), ("X3", 2, 0), ("Z2", 0, 1, 0), ("O2", 1, 1, 1), ("O2", 1, 1, 0),
        ("O2", 3, 1, 0), ("Z3", 0, 0, 0), ("Y1", 2, 1), ("M", 0, 1, 1), ("O2", 3, 1, 1), ("O2", 3, 0, 1),
        ("Y1", 2, 0), ("Z3", 0, 1, 0), ("Z0", 0, 1, 1), ("M", 0, 0, 1), ("Y2", 0, 0, 0), ("Z0", 0, 0, 1),
        ("Z2", 0, 1, 1), ("Y2", 0, 1, 0), ("A2", 2, 1), ("A2", 2, 0), ("M", 2, 1, 0), ("O2", 0, 0, 0),
        ("M", 2, 0, 0), ("Z0", 2, 1, 0), ("Z3", 0, 1, 1), ("Z2", 0, 0, 1), ("O3", 3, 0, 1), ("Z0", 2, 0, 0),
        ("O2", 0, 1, 0), ("M", 2, 0, 1), ("Z2", 2, 1, 0), ("M", 2, 1, 1), ("Z0", 2, 0, 1), ("Z2", 2, 0, 0),
        ("O3", 3, 1, 1), ("Z3", 0, 0, 1), ("O3", 0, 1, 0), ("Z0", 2, 1, 1), ("O3", 3, 1, 0), ("Z3", 2, 1, 0),
        ("Z2", 2, 0, 1), ("O3", 0, 0, 0), ("Y2", 0, 1, 1), ("Z3", 2, 0, 0), ("Z2", 2, 1, 1), ("E", 0, 1, 0),
        ("E", 3, 1, 1), ("Y2", 0, 0, 1), ("O3", 1, 1, 1), ("Y2", 2, 1, 0), ("Z3", 2, 0, 1), ("Z3", 2, 1, 1),
        ("Y2", 2, 0, 0), ("E", 3, 1, 0), ("E", 1, 0, 0), ("O2", 0, 0, 1), ("O3", 3, 0, 0), ("Y2", 2, 0, 1),
        ("Y2", 2, 1, 1), ("O2", 2, 1, 0), ("O3", 1, 1, 0), ("O3", 1, 0, 1), ("E", 3, 0, 1), ("O2", 2, 0, 0),
        ("O2", 2, 0, 1), ("O2", 0, 1, 1), ("O3", 0, 0, 1), ("E", 1, 1, 0), ("O2", 2, 1, 1), ("O3", 2, 1, 0),
        ("O3", 2, 0, 0), ("E", 0, 0, 0), ("O3", 2, 0, 1), ("E", 1, 0, 1), ("O3", 0, 1, 1), ("E", 2, 0, 0),
        ("E", 3, 0, 0), ("O3", 2, 1, 1), ("E", 0, 0, 1), ("E", 1, 1, 1), ("E", 2, 0, 1), ("E", 0, 1, 1),
        ("E", 2, 1, 0), ("E", 2, 1, 1),
    ]


def kernel(
    g, mst, mom, sqr, gate, up,
    mst_v, out,
    gv, r1, r2, sy, ry, mom_v, sqr_v, w, gate_v, up_v, hid,
    p, rc, zr1, zr2, yb, yr,
    lg, ld,
    x1s, x1r, rws, rwr, x2s, x2r, ys, yrs, a1s, a1r, a2s, a2r, hs, hr,
    cs, cr, z1s, z1r, zws, zwr, z2s, z2r, y3s, y3r, o1s, o1r, o2s, o2r, ocs, ocr,
):
    dp, t = lax.axis_index("dp"), lax.axis_index("tensor")
    x, yl = lax.div(dp, 2), lax.rem(dp, 2)
    z, yh, c = lax.div(t, 4), lax.rem(lax.div(t, 2), 2), lax.rem(t, 2)
    xn, xp = lax.rem(x + 1, 4), lax.rem(x + 3, 4)
    xo = lax.rem(x + 2, 4)
    zn, zp = lax.rem(z + 1, 4), lax.rem(z + 3, 4)
    zo = lax.rem(z + 2, 4)

    def dev(x=x, yl=yl, z=z, yh=yh, c=c):
        return (x * 2 + yl, z * 4 + yh * 2 + c)

    X = (dev(x=xn), dev(x=xp))
    Z = (dev(z=zn), dev(z=zp))
    YL = dev(yl=1 - yl)
    YH = dev(yh=1 - yh)
    YD = dev(yl=1 - yl, yh=1 - yh)
    C = dev(c=1 - c)

    rows = gv.shape[3]
    half = rows // 2
    tokens = hid.shape[1]
    core_rows = tokens // 2
    zrows = core_rows // 4
    zh = zrows // 2

    done = {}
    seen = set()
    settled = []
    step_at = [0]

    def arrive(*keys):
        for key in keys:
            if key not in seen:
                seen.add(key)
                done[key].wait_recv()
                settled.append((step_at[0], done[key]))

    def remote(src, dst, s, r, to):
        cp = pltpu.make_async_remote_copy(
            src_ref=src, dst_ref=dst, send_sem=s, recv_sem=r, device_id=to, device_id_type=MESH
        )
        cp.start()
        return cp

    def columns(owner, strip, k, width=LANES):
        return pl.ds(pl.multiple_of(owner * (2 * K * LANES) + strip * (K * LANES) + k * LANES, LANES), width)

    loads = {}
    ready = set()

    def load(name, sem, src, dst):
        cp = pltpu.make_async_copy(src, dst, sem)
        cp.start()
        loads[name] = cp

    def loaded(*names):
        for n in names:
            if n not in ready:
                ready.add(n)
                loads.pop(n).wait()

    owners = (x, xn, xo, xp)

    def loadg(k):
        for o, strip in ((2, 0), (2, 1), (1, 1), (3, 0), (1, 0), (3, 1), (0, 0), (0, 1)):
            load(("g", o, strip, k), lg.at[o, strip, k], g.at[0, :, columns(owners[o], strip, k)], gv.at[o, strip, k])

    chunks = [step[1] for step in plan() if step[0] == "X1"]
    loadg(chunks[0])
    load("gate", ld.at[0], gate, gate_v)
    load("up", ld.at[1], up, up_v)

    def L(i):
        if i == 0:
            loadg(chunks[1])
        elif i == 1:
            loadg(chunks[2])
            loadg(chunks[3])
        else:
            load("mst", ld.at[2], mst, mst_v)
            load("mom", ld.at[3], mom, mom_v)
            load("sqr", ld.at[4], sqr, sqr_v)

    barrier = pltpu.get_barrier_semaphore()
    friends = (*X, *Z, YL, YH, YD, C)
    for d in friends:
        pl.semaphore_signal(barrier, inc=1, device_id=d, device_id_type=MESH)
    pl.semaphore_wait(barrier, len(friends))

    def X1(k):
        for d in (0, 1):
            loaded(("g", 2, d, k))
            done["x1", d, k] = remote(gv.at[2, d, k], r1.at[d, k], x1s.at[d, k], x1r.at[d, k], X[d])

    def R(k):
        for d, o in ((0, 1), (1, 3)):
            loaded(("g", o, 1 - d, k))
            done["rw", d, k] = remote(
                gv.at[o, 1 - d, k], r2.at[d, k, 1 - d], rws.at[d, k], rwr.at[d, k], X[d])

    def X2(k, part):
        at_part = pl.ds(part * half, half)
        for d, o in ((0, 1), (1, 3)):
            loaded(("g", o, d, k))
            arrive(("x1", d, k))

            def body(r):
                at = pl.ds(pl.multiple_of(part * half + r, 64), 64)
                gv[o, d, k, at, :] = (gv[o, d, k, at, :].astype(F32) + r1[d, k, at, :].astype(F32)).astype(BF16)

            sweep(half, 64, body)
            done["x2", d, k, part] = remote(
                gv.at[o, d, k, at_part], r2.at[d, k, d, at_part], x2s.at[d, k, part], x2r.at[d, k, part], X[d])

    def X3(k, part):
        loaded(("g", 0, 0, k), ("g", 0, 1, k))
        for d in (0, 1):
            arrive(("rw", d, k), ("x2", d, k, part))
        other = 1 - yl

        def body(r):
            at = pl.ds(pl.multiple_of(part * half + r, 64), 64)
            sy[k, at, :] = (
                gv[0, other, k, at, :].astype(F32)
                + r2[0, k, other, at, :].astype(F32)
                + r2[1, k, other, at, :].astype(F32)
            ).astype(BF16)

        sweep(half, 64, body)
        at_part = pl.ds(part * half, half)
        done["y", k, part] = remote(sy.at[k, at_part], ry.at[k, at_part], ys.at[k, part], yrs.at[k, part], YL)

    learn_rate = 0.8 / math.sqrt(FF)
    corr_one = 1.0 - beta_one**step_count
    corr_two = 1.0 - beta_two**step_count

    def Y1(k, part):
        loaded("mst", "mom", "sqr")
        arrive(("y", k, part))
        cols = pl.ds(k * LANES, LANES)

        def body(r):
            at = pl.ds(pl.multiple_of(part * half + r, 64), 64)
            grad = (
                gv[0, yl, k, at, :].astype(F32)
                + r2[0, k, yl, at, :].astype(F32)
                + r2[1, k, yl, at, :].astype(F32)
                + ry[k, at, :].astype(F32)
            )
            moment_new = beta_one * mom_v[at, cols] + (1.0 - beta_one) * grad
            square_new = beta_two * sqr_v[at, cols] + (1.0 - beta_two) * grad * grad
            update = moment_new / corr_one / (jnp.sqrt(square_new / corr_two) + epsilon)
            old = mst_v[at, cols]
            new = old - learn_rate * (update + weight_decay * old)
            mst_v[at, cols] = new
            w[k, 0, at, :] = new.astype(BF16)

        sweep(half, 64, body)
        at_part = pl.ds(part * half, half)
        for d in (0, 1):
            done["a1", d, k, part] = remote(
                w.at[k, 0, at_part], w.at[k, 2 - d, at_part], a1s.at[d, k, part], a1r.at[d, k, part], X[d])

    def A2(k, d):
        arrive(("a1", d, k, d))
        at = pl.ds(d * half, half)
        done["a2", d, k] = remote(
            w.at[k, 2 - d, at], w.at[k, 3, at], a2s.at[d, k], a2r.at[d, k], X[d])

    piece = tokens // HP

    def HID(i):
        loaded("gate", "up")

        def body(r):
            at = pl.ds(pl.multiple_of(i * piece + r, 32), 32)
            v = gate_v[at, :].astype(F32)
            hid[0, at, :] = (v / (1.0 + jnp.exp(-v)) * up_v[at, :].astype(F32)).astype(BF16)

        sweep(piece, 32, body)

    def H(i):
        at = pl.ds(i * piece, piece)
        done["h", i] = remote(hid.at[0, at], hid.at[1, at], hs.at[i], hr.at[i], YL)

    def M(k, h, q):
        arrive(*(("a1", d, k, part) for d in (0, 1) for part in (0, 1)))
        if q == 1:
            arrive(("a2", 0, k), ("a2", 1, k))
        if h == 1:
            arrive(*(("h", i) for i in range(HP)))
        for part in (1 - c, c):
            at = pl.ds(pl.multiple_of(part * core_rows, core_rows), core_rows)
            weights = jnp.concatenate([w[k, 2 * q], w[k, 2 * q + 1]], axis=1)
            p[k, h, q, at, :] = jnp.dot(
                hid[h, at, :], weights, preferred_element_type=F32).astype(BF16)
            if part is not c:
                done["c", k, h, q] = remote(p.at[k, h, q, at], rc.at[k, h, q], cs.at[k, h, q], cr.at[k, h, q], C)

    base = c * core_rows

    def zat(owner, part, count):
        return pl.ds(pl.multiple_of(base + owner * zrows + part * zh, zh), count)

    def Z0(k, h, q):
        arrive(("c", k, h, q))

        def body(r):
            at = pl.ds(pl.multiple_of(base + r, 128), 128)
            p[k, h, q, at, :] = (
                p[k, h, q, at, :].astype(F32) + rc[k, h, q, pl.ds(r, 128), :].astype(F32)).astype(BF16)

        sweep(core_rows, 128, body)
        for d in (0, 1):
            done["z1", d, k, h, q] = remote(
                p.at[k, h, q, zat(zo, d, zh)], zr1.at[d, k, h, q], z1s.at[d, k, h, q], z1r.at[d, k, h, q], Z[d])
        for d, owner in ((0, zn), (1, zp)):
            done["zw", d, k, h, q] = remote(
                p.at[k, h, q, zat(owner, 1 - d, zh)], zr2.at[d, k, h, q, pl.ds((1 - d) * zh, zh)],
                zws.at[d, k, h, q], zwr.at[d, k, h, q], Z[d])

    def Z2(k, h, q):
        for d, owner in ((0, zn), (1, zp)):
            arrive(("z1", d, k, h, q))
            at = zat(owner, d, zh)
            p[k, h, q, at, :] = (p[k, h, q, at, :].astype(F32) + zr1[d, k, h, q].astype(F32)).astype(BF16)
            done["z2", d, k, h, q] = remote(
                p.at[k, h, q, at], zr2.at[d, k, h, q, pl.ds(d * zh, zh)], z2s.at[d, k, h, q], z2r.at[d, k, h, q], Z[d])

    def Z3(k, h, q):
        for d in (0, 1):
            arrive(("zw", d, k, h, q), ("z2", d, k, h, q))
        for part in (0, 1):
            at = pl.ds(part * zh, zh)
            yb[k, h, q, at, :] = (
                p[k, h, q, zat(z, part, zh), :].astype(F32)
                + zr2[0, k, h, q, at, :].astype(F32)
                + zr2[1, k, h, q, at, :].astype(F32)
            ).astype(BF16)
        for i, to in ((0, YH),) if h == 0 else ((1, YL), (2, YD)):
            done["y3", i, k, q] = remote(yb.at[k, h, q], yr.at[i, k, q], y3s.at[i, k, q], y3r.at[i, k, q], to)

    def Y2(k, h, q):
        group = yl if h == 0 else 1 - yl
        arrive(*(("y3", i, k, q) for i in ((0,) if h == 0 else (1, 2))))
        for part in (0, 1):
            at = pl.ds(part * zh, zh)
            if h == 0:
                total = yb[k, 0, q, at, :].astype(F32) + yr[0, k, q, at, :].astype(F32)
            else:
                total = yr[1, k, q, at, :].astype(F32) + yr[2, k, q, at, :].astype(F32)
            out[k, group, q, zat(z, part, zh), :] = total.astype(BF16)
        mine = out.at[k, group, q, zat(z, 0, zrows)]
        for d in (0, 1):
            done["o1", d, k, h, q] = remote(mine, mine, o1s.at[d, k, h, q], o1r.at[d, k, h, q], Z[d])

    def O2(k, h, q):
        group = yl if h == 0 else 1 - yl
        for d, origin in ((0, zp), (1, zn)):
            arrive(("o1", d, k, h, q))
            part = out.at[k, group, q, zat(origin, d, zh)]
            done["o2", d, k, h, q] = remote(part, part, o2s.at[d, k, h, q], o2r.at[d, k, h, q], Z[d])

    def O3(k, h, q):
        group = yl if h == 0 else 1 - yl
        arrive(("o2", 0, k, h, q), ("o2", 1, k, h, q))
        part = out.at[k, group, q, pl.ds(pl.multiple_of(base, core_rows), core_rows)]
        done["oc", k, h, q] = remote(part, part, ocs.at[k, h, q], ocr.at[k, h, q], C)

    def E(k, h, q):
        arrive(("oc", k, h, q))

    steps = dict(L=L, X1=X1, R=R, X2=X2, X3=X3, Y1=Y1, A2=A2, HID=HID, H=H, M=M, Z0=Z0, Z2=Z2, Z3=Z3, Y2=Y2, O2=O2, O3=O3, E=E)
    for number, (name, *at) in enumerate(plan()):
        step_at[0] = number
        steps[name](*at)
        while settled and settled[0][0] <= number - LATER:
            settled.pop(0)[1].wait_send()

    for _, cp in settled:
        cp.wait_send()


def place(nm, out, nm_out, mix_out, sems):
    x = lax.div(lax.axis_index("dp"), 2)
    copies = [pltpu.make_async_copy(nm, nm_out, sems.at[0])]
    for k in range(K):
        for group in (0, 1):
            for slot, ahead in enumerate((0, 1, 3, 2)):
                owner = lax.rem(x + ahead, 4)
                at = pl.ds(pl.multiple_of((owner * 2 * K + group * K + k) * LANES, LANES), LANES)
                copies.append(pltpu.make_async_copy(
                    out.at[k, group, slot // 2, :, pl.ds(slot % 2 * LANES, LANES)],
                    mix_out.at[:, at], sems.at[len(copies)]))
    for cp in copies:
        cp.start()
    for cp in copies:
        cp.wait()


def per_device(grad_parts, master, moment_one, moment_two, gate_act, up_act):
    _, rows, width = grad_parts.shape
    tokens = gate_act.shape[0]
    hbm = pl.BlockSpec(memory_space=pl.ANY)
    block = K * LANES
    vm = pltpu.VMEM
    dma = pltpu.SemaphoreType.DMA

    def pair(shape):
        return [dma(shape), dma(shape)]

    new_master, mixed = pl.pallas_call(
        kernel,
        out_shape=(
            vm(master.shape, F32),
            vm((K, 2, 2, tokens, block // 2), BF16),
        ),
        in_specs=[hbm] * 6,
        scratch_shapes=[
            vm((4, 2, K, rows, LANES), BF16),
            vm((2, K, rows, LANES), BF16),
            vm((2, K, 2, rows, LANES), BF16),
            vm((K, rows, LANES), BF16),
            vm((K, rows, LANES), BF16),
            vm((rows, block), F32),
            vm((rows, block), F32),
            vm((K, 4, rows, LANES), BF16),
            vm((tokens, rows), BF16),
            vm((tokens, rows), BF16),
            vm((2, tokens, rows), BF16),
            vm((K, 2, 2, tokens, block // 2), BF16),
            vm((K, 2, 2, tokens // 2, block // 2), BF16),
            vm((2, K, 2, 2, tokens // 16, block // 2), BF16),
            vm((2, K, 2, 2, tokens // 8, block // 2), BF16),
            vm((K, 2, 2, tokens // 8, block // 2), BF16),
            vm((3, K, 2, tokens // 8, block // 2), BF16),
            dma((4, 2, K)), dma((5,)),
            *pair((2, K)), *pair((2, K)), *pair((2, K, 2)), *pair((K, 2)),
            *pair((2, K, 2)), *pair((2, K)), *pair((HP,)),
            *pair((K, 2, 2)), *pair((2, K, 2, 2)), *pair((2, K, 2, 2)), *pair((2, K, 2, 2)),
            *pair((3, K, 2)), *pair((2, K, 2, 2)), *pair((2, K, 2, 2)), *pair((K, 2, 2)),
        ],
        compiler_params=pltpu.CompilerParams(
            collective_id=0, has_side_effects=True, vmem_limit_bytes=50 * 2**20
        ),
        name="handover",
    )(grad_parts, master, moment_one, moment_two, gate_act, up_act)
    return pl.pallas_call(
        place,
        out_shape=(
            jax.ShapeDtypeStruct(master.shape, F32),
            jax.ShapeDtypeStruct((tokens, width), BF16),
        ),
        in_specs=[hbm] * 2,
        out_specs=(hbm, hbm),
        scratch_shapes=[dma((1 + 8 * K,))],
        compiler_params=pltpu.CompilerParams(vmem_limit_bytes=2**20),
        name="place",
    )(pltpu.with_memory_space_constraint(new_master, vm), pltpu.with_memory_space_constraint(mixed, vm))


def solution(mesh):
    in_specs = (
        P("dp", "tensor", None),
        P("tensor", "dp"),
        P("tensor", "dp"),
        P("tensor", "dp"),
        P("dp", "tensor"),
        P("dp", "tensor"),
    )
    out_specs = (P("tensor", "dp"), P("dp", None))
    return jax.shard_map(
        per_device, mesh=mesh, in_specs=in_specs, out_specs=out_specs, check_vma=False
    )
```

```python
import functools
import math

import jax
import jax.numpy as jnp
from jax import lax
from jax.experimental import pallas as pl
from jax.experimental.pallas import tpu as pltpu
from jax.sharding import PartitionSpec as P

FF = 14336

beta_one = 0.9
beta_two = 0.95
epsilon = 1e-08
weight_decay = 0.1
step_count = 20

MESH = pl.DeviceIdType.MESH
F32 = jnp.float32
BF16 = jnp.bfloat16

K = 4
LANES = 128
HP = 8
LATER = 6


def sweep(rows, tile, body):
    if rows == tile:
        body(0)
        return

    @pl.loop(0, rows // tile)
    def _(i):
        body(pl.multiple_of(i * tile, tile))


def plan():
    return [
        ("X1", 3), ("HID", 6), ("R", 3), ("L", 0), ("H", 6), ("HID", 4), ("HID", 7), ("L", 1), ("H", 7),
        ("HID", 0), ("X2", 3, 1), ("X1", 1), ("H", 0), ("HID", 2), ("L", 2), ("H", 2), ("X3", 3, 1), ("HID", 1),
        ("HID", 5), ("X2", 3, 0), ("R", 1), ("X2", 1, 0), ("X3", 3, 0), ("X2", 1, 1), ("H", 1), ("Y1", 3, 1),
        ("HID", 3), ("Y1", 3, 0), ("H", 3), ("X1", 0), ("X3", 1, 0), ("X3", 1, 1), ("A2", 3, 1), ("M", 3, 0, 0),
        ("H", 5), ("A2", 3, 0), ("Z0", 3, 0, 0), ("H", 4), ("Y1", 1, 0), ("Y1", 1, 1), ("Z2", 3, 0, 0),
        ("R", 0), ("M", 3, 0, 1), ("X2", 0, 0), ("Z0", 3, 0, 1), ("M", 1, 0, 0), ("X2", 0, 1), ("Z3", 3, 0, 0),
        ("Z2", 3, 0, 1), ("Z0", 1, 0, 0), ("M", 3, 1, 0), ("M", 3, 1, 1), ("Z3", 3, 0, 1), ("Z2", 1, 0, 0),
        ("Z0", 3, 1, 0), ("A2", 1, 0), ("A2", 1, 1), ("X1", 2), ("X3", 0, 0), ("Y2", 3, 0, 0), ("M", 1, 1, 0),
        ("Z0", 3, 1, 1), ("X3", 0, 1), ("Z0", 1, 1, 0), ("Y2", 3, 0, 1), ("Z2", 3, 1, 0), ("Z3", 1, 0, 0),
        ("M", 1, 0, 1), ("Z2", 3, 1, 1), ("Y1", 0, 0), ("Z2", 1, 1, 0), ("Z0", 1, 0, 1), ("Y1", 0, 1),
        ("M", 1, 1, 1), ("Y2", 1, 0, 0), ("Z3", 3, 1, 1), ("X2", 2, 0), ("O2", 3, 0, 0), ("Z3", 1, 1, 0),
        ("R", 2), ("Z2", 1, 0, 1), ("Z0", 1, 1, 1), ("X2", 2, 1), ("Z3", 3, 1, 0), ("O2", 1, 0, 0),
        ("Y2", 3, 1, 1), ("M", 0, 0, 0), ("Z2", 1, 1, 1), ("Y2", 1, 1, 0), ("M", 0, 1, 0), ("Z3", 1, 0, 1),
        ("Z0", 0, 0, 0), ("A2", 0, 1), ("Z0", 0, 1, 0), ("Z3", 1, 1, 1), ("Y2", 3, 1, 0), ("O2", 1, 1, 0),
        ("A2", 0, 0), ("O3", 1, 0, 0), ("X3", 2, 0), ("Z2", 0, 0, 0), ("O3", 3, 0, 0), ("Y2", 1, 1, 1),
        ("X3", 2, 1), ("Y2", 1, 0, 1), ("Z2", 0, 1, 0), ("O2", 3, 1, 1), ("O2", 3, 0, 1), ("O2", 3, 1, 0),
        ("Z3", 0, 0, 0), ("Y1", 2, 0), ("M", 0, 0, 1), ("O2", 1, 1, 1), ("Y1", 2, 1), ("O2", 1, 0, 1),
        ("Z3", 0, 1, 0), ("Z0", 0, 0, 1), ("M", 0, 1, 1), ("A2", 2, 0), ("Y2", 0, 0, 0), ("Z0", 0, 1, 1),
        ("Z2", 0, 0, 1), ("Y2", 0, 1, 0), ("A2", 2, 1), ("M", 2, 0, 0), ("M", 2, 1, 0), ("Z0", 2, 0, 0),
        ("O3", 3, 1, 0), ("Z3", 0, 0, 1), ("Z2", 0, 1, 1), ("O2", 0, 0, 0), ("Z0", 2, 1, 0), ("M", 2, 1, 1),
        ("Z2", 2, 0, 0), ("M", 2, 0, 1), ("Z0", 2, 1, 1), ("Z3", 0, 1, 1), ("Z0", 2, 0, 1), ("O3", 1, 1, 1),
        ("Z2", 2, 1, 0), ("O3", 3, 0, 1), ("O3", 0, 0, 0), ("Z2", 2, 1, 1), ("Z3", 2, 0, 0), ("Y2", 0, 0, 1),
        ("Z2", 2, 0, 1), ("Z3", 2, 1, 0), ("Y2", 0, 1, 1), ("Z3", 2, 1, 1), ("O2", 0, 1, 0), ("O3", 1, 0, 1),
        ("O3", 1, 1, 0), ("Y2", 2, 0, 0), ("O3", 3, 1, 1), ("O2", 0, 0, 1), ("Z3", 2, 0, 1), ("E", 3, 0, 1),
        ("Y2", 2, 1, 0), ("Y2", 2, 1, 1), ("Y2", 2, 0, 1), ("O2", 2, 1, 0), ("O3", 0, 1, 0), ("O3", 0, 0, 1),
        ("E", 1, 0, 1), ("O2", 0, 1, 1), ("E", 3, 1, 1), ("O2", 2, 0, 0), ("O2", 2, 1, 1), ("E", 0, 0, 1),
        ("O2", 2, 0, 1), ("O3", 2, 1, 0), ("O3", 0, 1, 1), ("E", 1, 1, 0), ("O3", 2, 0, 0), ("E", 0, 1, 0),
        ("E", 3, 0, 0), ("E", 2, 1, 0), ("E", 1, 1, 1), ("E", 0, 0, 0), ("O3", 2, 1, 1), ("E", 3, 1, 0),
        ("E", 1, 0, 0), ("O3", 2, 0, 1), ("E", 0, 1, 1), ("E", 2, 0, 0), ("E", 2, 1, 1), ("E", 2, 0, 1),
    ]


def kernel(
    g, mst, mom, sqr, gate, up,
    mst_v, out,
    gv, r1, r2, sy, ry, mom_v, sqr_v, w, gate_v, up_v, hid,
    p, rc, zr1, zr2, yb, yr,
    lg, ld,
    x1s, x1r, rws, rwr, x2s, x2r, ys, yrs, a1s, a1r, a2s, a2r, hs, hr,
    cs, cr, z1s, z1r, zws, zwr, z2s, z2r, y3s, y3r, o1s, o1r, o2s, o2r, ocs, ocr,
):
    dp, t = lax.axis_index("dp"), lax.axis_index("tensor")
    x, yl = lax.div(dp, 2), lax.rem(dp, 2)
    z, yh, c = lax.div(t, 4), lax.rem(lax.div(t, 2), 2), lax.rem(t, 2)
    xn, xp = lax.rem(x + 1, 4), lax.rem(x + 3, 4)
    xo = lax.rem(x + 2, 4)
    zn, zp = lax.rem(z + 1, 4), lax.rem(z + 3, 4)
    zo = lax.rem(z + 2, 4)

    def dev(x=x, yl=yl, z=z, yh=yh, c=c):
        return (x * 2 + yl, z * 4 + yh * 2 + c)

    X = (dev(x=xn), dev(x=xp))
    Z = (dev(z=zn), dev(z=zp))
    YL = dev(yl=1 - yl)
    YH = dev(yh=1 - yh)
    YD = dev(yl=1 - yl, yh=1 - yh)
    C = dev(c=1 - c)

    rows = gv.shape[3]
    half = rows // 2
    tokens = hid.shape[1]
    core_rows = tokens // 2
    zrows = core_rows // 4
    zh = zrows // 2

    done = {}
    seen = set()
    settled = []
    step_at = [0]

    def arrive(*keys):
        for key in keys:
            if key not in seen:
                seen.add(key)
                done[key].wait_recv()
                settled.append((step_at[0], done[key]))

    def remote(src, dst, s, r, to):
        cp = pltpu.make_async_remote_copy(
            src_ref=src, dst_ref=dst, send_sem=s, recv_sem=r, device_id=to, device_id_type=MESH
        )
        cp.start()
        return cp

    def columns(owner, strip, k, width=LANES):
        return pl.ds(pl.multiple_of(owner * (2 * K * LANES) + strip * (K * LANES) + k * LANES, LANES), width)

    loads = {}
    ready = set()

    def load(name, sem, src, dst):
        cp = pltpu.make_async_copy(src, dst, sem)
        cp.start()
        loads[name] = cp

    def loaded(*names):
        for n in names:
            if n not in ready:
                ready.add(n)
                loads.pop(n).wait()

    owners = (x, xn, xo, xp)

    def loadg(k):
        for o, strip in ((2, 0), (2, 1), (1, 1), (3, 0), (1, 0), (3, 1), (0, 0), (0, 1)):
            load(("g", o, strip, k), lg.at[o, strip, k], g.at[0, :, columns(owners[o], strip, k)], gv.at[o, strip, k])

    chunks = [step[1] for step in plan() if step[0] == "X1"]
    loadg(chunks[0])
    load("gate", ld.at[0], gate, gate_v)
    load("up", ld.at[1], up, up_v)

    def L(i):
        if i == 0:
            loadg(chunks[1])
        elif i == 1:
            loadg(chunks[2])
            loadg(chunks[3])
        else:
            load("mst", ld.at[2], mst, mst_v)
            load("mom", ld.at[3], mom, mom_v)
            load("sqr", ld.at[4], sqr, sqr_v)

    barrier = pltpu.get_barrier_semaphore()
    friends = (*X, *Z, YL, YH, YD, C)
    for d in friends:
        pl.semaphore_signal(barrier, inc=1, device_id=d, device_id_type=MESH)
    pl.semaphore_wait(barrier, len(friends))

    def X1(k):
        for d in (0, 1):
            loaded(("g", 2, d, k))
            done["x1", d, k] = remote(gv.at[2, d, k], r1.at[d, k], x1s.at[d, k], x1r.at[d, k], X[d])

    def R(k):
        for d, o in ((0, 1), (1, 3)):
            loaded(("g", o, 1 - d, k))
            done["rw", d, k] = remote(
                gv.at[o, 1 - d, k], r2.at[d, k, 1 - d], rws.at[d, k], rwr.at[d, k], X[d])

    def X2(k, part):
        at_part = pl.ds(part * half, half)
        for d, o in ((0, 1), (1, 3)):
            loaded(("g", o, d, k))
            arrive(("x1", d, k))

            def body(r):
                at = pl.ds(pl.multiple_of(part * half + r, 64), 64)
                gv[o, d, k, at, :] = (gv[o, d, k, at, :].astype(F32) + r1[d, k, at, :].astype(F32)).astype(BF16)

            sweep(half, 64, body)
            done["x2", d, k, part] = remote(
                gv.at[o, d, k, at_part], r2.at[d, k, d, at_part], x2s.at[d, k, part], x2r.at[d, k, part], X[d])

    def X3(k, part):
        loaded(("g", 0, 0, k), ("g", 0, 1, k))
        for d in (0, 1):
            arrive(("rw", d, k), ("x2", d, k, part))
        other = 1 - yl

        def body(r):
            at = pl.ds(pl.multiple_of(part * half + r, 64), 64)
            sy[k, at, :] = (
                gv[0, other, k, at, :].astype(F32)
                + r2[0, k, other, at, :].astype(F32)
                + r2[1, k, other, at, :].astype(F32)
            ).astype(BF16)

        sweep(half, 64, body)
        at_part = pl.ds(part * half, half)
        done["y", k, part] = remote(sy.at[k, at_part], ry.at[k, at_part], ys.at[k, part], yrs.at[k, part], YL)

    learn_rate = 0.8 / math.sqrt(FF)
    corr_one = 1.0 - beta_one**step_count
    corr_two = 1.0 - beta_two**step_count

    def Y1(k, part):
        loaded("mst", "mom", "sqr")
        arrive(("y", k, part))
        cols = pl.ds(k * LANES, LANES)

        def body(r):
            at = pl.ds(pl.multiple_of(part * half + r, 64), 64)
            grad = (
                gv[0, yl, k, at, :].astype(F32)
                + r2[0, k, yl, at, :].astype(F32)
                + r2[1, k, yl, at, :].astype(F32)
                + ry[k, at, :].astype(F32)
            )
            moment_new = beta_one * mom_v[at, cols] + (1.0 - beta_one) * grad
            square_new = beta_two * sqr_v[at, cols] + (1.0 - beta_two) * grad * grad
            update = moment_new / corr_one / (jnp.sqrt(square_new / corr_two) + epsilon)
            old = mst_v[at, cols]
            new = old - learn_rate * (update + weight_decay * old)
            mst_v[at, cols] = new
            w[k, 0, at, :] = new.astype(BF16)

        sweep(half, 64, body)
        at_part = pl.ds(part * half, half)
        for d in (0, 1):
            done["a1", d, k, part] = remote(
                w.at[k, 0, at_part], w.at[k, 2 - d, at_part], a1s.at[d, k, part], a1r.at[d, k, part], X[d])

    def A2(k, d):
        arrive(("a1", d, k, d))
        at = pl.ds(d * half, half)
        done["a2", d, k] = remote(
            w.at[k, 2 - d, at], w.at[k, 3, at], a2s.at[d, k], a2r.at[d, k], X[d])

    piece = tokens // HP

    def HID(i):
        loaded("gate", "up")

        def body(r):
            at = pl.ds(pl.multiple_of(i * piece + r, 32), 32)
            v = gate_v[at, :].astype(F32)
            hid[0, at, :] = (v / (1.0 + jnp.exp(-v)) * up_v[at, :].astype(F32)).astype(BF16)

        sweep(piece, 32, body)

    def H(i):
        at = pl.ds(i * piece, piece)
        done["h", i] = remote(hid.at[0, at], hid.at[1, at], hs.at[i], hr.at[i], YL)

    def M(k, h, q):
        arrive(*(("a1", d, k, part) for d in (0, 1) for part in (0, 1)))
        if q == 1:
            arrive(("a2", 0, k), ("a2", 1, k))
        if h == 1:
            arrive(*(("h", i) for i in range(HP)))
        for part in (1 - c, c):
            at = pl.ds(pl.multiple_of(part * core_rows, core_rows), core_rows)
            weights = jnp.concatenate([w[k, 2 * q], w[k, 2 * q + 1]], axis=1)
            p[k, h, q, at, :] = jnp.dot(
                hid[h, at, :], weights, preferred_element_type=F32).astype(BF16)
            if part is not c:
                done["c", k, h, q] = remote(p.at[k, h, q, at], rc.at[k, h, q], cs.at[k, h, q], cr.at[k, h, q], C)

    base = c * core_rows

    def zat(owner, part, count):
        return pl.ds(pl.multiple_of(base + owner * zrows + part * zh, zh), count)

    def Z0(k, h, q):
        arrive(("c", k, h, q))

        def body(r):
            at = pl.ds(pl.multiple_of(base + r, 128), 128)
            p[k, h, q, at, :] = (
                p[k, h, q, at, :].astype(F32) + rc[k, h, q, pl.ds(r, 128), :].astype(F32)).astype(BF16)

        sweep(core_rows, 128, body)
        for d in (0, 1):
            done["z1", d, k, h, q] = remote(
                p.at[k, h, q, zat(zo, d, zh)], zr1.at[d, k, h, q], z1s.at[d, k, h, q], z1r.at[d, k, h, q], Z[d])
        for d, owner in ((0, zn), (1, zp)):
            done["zw", d, k, h, q] = remote(
                p.at[k, h, q, zat(owner, 1 - d, zh)], zr2.at[d, k, h, q, pl.ds((1 - d) * zh, zh)],
                zws.at[d, k, h, q], zwr.at[d, k, h, q], Z[d])

    def Z2(k, h, q):
        for d, owner in ((0, zn), (1, zp)):
            arrive(("z1", d, k, h, q))
            at = zat(owner, d, zh)
            p[k, h, q, at, :] = (p[k, h, q, at, :].astype(F32) + zr1[d, k, h, q].astype(F32)).astype(BF16)
            done["z2", d, k, h, q] = remote(
                p.at[k, h, q, at], zr2.at[d, k, h, q, pl.ds(d * zh, zh)], z2s.at[d, k, h, q], z2r.at[d, k, h, q], Z[d])

    def Z3(k, h, q):
        for d in (0, 1):
            arrive(("zw", d, k, h, q), ("z2", d, k, h, q))
        for part in (0, 1):
            at = pl.ds(part * zh, zh)
            yb[k, h, q, at, :] = (
                p[k, h, q, zat(z, part, zh), :].astype(F32)
                + zr2[0, k, h, q, at, :].astype(F32)
                + zr2[1, k, h, q, at, :].astype(F32)
            ).astype(BF16)
        for i, to in ((0, YH),) if h == 0 else ((1, YL), (2, YD)):
            done["y3", i, k, q] = remote(yb.at[k, h, q], yr.at[i, k, q], y3s.at[i, k, q], y3r.at[i, k, q], to)

    def Y2(k, h, q):
        group = yl if h == 0 else 1 - yl
        arrive(*(("y3", i, k, q) for i in ((0,) if h == 0 else (1, 2))))
        for part in (0, 1):
            at = pl.ds(part * zh, zh)
            if h == 0:
                total = yb[k, 0, q, at, :].astype(F32) + yr[0, k, q, at, :].astype(F32)
            else:
                total = yr[1, k, q, at, :].astype(F32) + yr[2, k, q, at, :].astype(F32)
            out[k, group, q, zat(z, part, zh), :] = total.astype(BF16)
        mine = out.at[k, group, q, zat(z, 0, zrows)]
        for d in (0, 1):
            done["o1", d, k, h, q] = remote(mine, mine, o1s.at[d, k, h, q], o1r.at[d, k, h, q], Z[d])

    def O2(k, h, q):
        group = yl if h == 0 else 1 - yl
        for d, origin in ((0, zp), (1, zn)):
            arrive(("o1", d, k, h, q))
            part = out.at[k, group, q, zat(origin, d, zh)]
            done["o2", d, k, h, q] = remote(part, part, o2s.at[d, k, h, q], o2r.at[d, k, h, q], Z[d])

    def O3(k, h, q):
        group = yl if h == 0 else 1 - yl
        arrive(("o2", 0, k, h, q), ("o2", 1, k, h, q))
        part = out.at[k, group, q, pl.ds(pl.multiple_of(base, core_rows), core_rows)]
        done["oc", k, h, q] = remote(part, part, ocs.at[k, h, q], ocr.at[k, h, q], C)

    def E(k, h, q):
        arrive(("oc", k, h, q))

    steps = dict(L=L, X1=X1, R=R, X2=X2, X3=X3, Y1=Y1, A2=A2, HID=HID, H=H, M=M, Z0=Z0, Z2=Z2, Z3=Z3, Y2=Y2, O2=O2, O3=O3, E=E)
    for number, (name, *at) in enumerate(plan()):
        step_at[0] = number
        steps[name](*at)
        while settled and settled[0][0] <= number - LATER:
            settled.pop(0)[1].wait_send()

    for _, cp in settled:
        cp.wait_send()


def place(nm, out, nm_out, mix_out, sems):
    x = lax.div(lax.axis_index("dp"), 2)
    copies = [pltpu.make_async_copy(nm, nm_out, sems.at[0])]
    for k in range(K):
        for group in (0, 1):
            for slot, ahead in enumerate((0, 1, 3, 2)):
                owner = lax.rem(x + ahead, 4)
                at = pl.ds(pl.multiple_of((owner * 2 * K + group * K + k) * LANES, LANES), LANES)
                copies.append(pltpu.make_async_copy(
                    out.at[k, group, slot // 2, :, pl.ds(slot % 2 * LANES, LANES)],
                    mix_out.at[:, at], sems.at[len(copies)]))
    for cp in copies:
        cp.start()
    for cp in copies:
        cp.wait()


def per_device(grad_parts, master, moment_one, moment_two, gate_act, up_act):
    _, rows, width = grad_parts.shape
    tokens = gate_act.shape[0]
    hbm = pl.BlockSpec(memory_space=pl.ANY)
    block = K * LANES
    vm = pltpu.VMEM
    dma = pltpu.SemaphoreType.DMA

    def pair(shape):
        return [dma(shape), dma(shape)]

    new_master, mixed = pl.pallas_call(
        kernel,
        out_shape=(
            vm(master.shape, F32),
            vm((K, 2, 2, tokens, block // 2), BF16),
        ),
        in_specs=[hbm] * 6,
        scratch_shapes=[
            vm((4, 2, K, rows, LANES), BF16),
            vm((2, K, rows, LANES), BF16),
            vm((2, K, 2, rows, LANES), BF16),
            vm((K, rows, LANES), BF16),
            vm((K, rows, LANES), BF16),
            vm((rows, block), F32),
            vm((rows, block), F32),
            vm((K, 4, rows, LANES), BF16),
            vm((tokens, rows), BF16),
            vm((tokens, rows), BF16),
            vm((2, tokens, rows), BF16),
            vm((K, 2, 2, tokens, block // 2), BF16),
            vm((K, 2, 2, tokens // 2, block // 2), BF16),
            vm((2, K, 2, 2, tokens // 16, block // 2), BF16),
            vm((2, K, 2, 2, tokens // 8, block // 2), BF16),
            vm((K, 2, 2, tokens // 8, block // 2), BF16),
            vm((3, K, 2, tokens // 8, block // 2), BF16),
            dma((4, 2, K)), dma((5,)),
            *pair((2, K)), *pair((2, K)), *pair((2, K, 2)), *pair((K, 2)),
            *pair((2, K, 2)), *pair((2, K)), *pair((HP,)),
            *pair((K, 2, 2)), *pair((2, K, 2, 2)), *pair((2, K, 2, 2)), *pair((2, K, 2, 2)),
            *pair((3, K, 2)), *pair((2, K, 2, 2)), *pair((2, K, 2, 2)), *pair((K, 2, 2)),
        ],
        compiler_params=pltpu.CompilerParams(
            collective_id=0, has_side_effects=True, vmem_limit_bytes=50 * 2**20
        ),
        name="handover",
    )(grad_parts, master, moment_one, moment_two, gate_act, up_act)
    return pl.pallas_call(
        place,
        out_shape=(
            jax.ShapeDtypeStruct(master.shape, F32),
            jax.ShapeDtypeStruct((tokens, width), BF16),
        ),
        in_specs=[hbm] * 2,
        out_specs=(hbm, hbm),
        scratch_shapes=[dma((1 + 8 * K,))],
        compiler_params=pltpu.CompilerParams(vmem_limit_bytes=2**20),
        name="place",
    )(pltpu.with_memory_space_constraint(new_master, vm), pltpu.with_memory_space_constraint(mixed, vm))


def solution(mesh):
    in_specs = (
        P("dp", "tensor", None),
        P("tensor", "dp"),
        P("tensor", "dp"),
        P("tensor", "dp"),
        P("dp", "tensor"),
        P("dp", "tensor"),
    )
    out_specs = (P("tensor", "dp"), P("dp", None))
    return jax.shard_map(
        per_device, mesh=mesh, in_specs=in_specs, out_specs=out_specs, check_vma=False
    )
```
